256 devices in a mesh: section: 8 (over y_hi, x), seq: 32 (over z, y_lo, core).
Axes of the slice: x: 4, y: 4 (y_hi: 2, y_lo: 2; y = y_hi * 2 + y_lo), z: 8, core: 2. Of those that a mesh axis runs over, the one named last changes fastest.
Arguments:
- text_embed: bfloat16 [98304, 8192], P('seq', 'section')
- vis_rows: bfloat16 [90112, 8192], P('seq', 'section')
- norm_gain: bfloat16 [8192], P('section'), may hold values from 0.25 to 1.75
- w_kv: bfloat16 [8192, 1024], P('section', 'seq'), may hold values from -0.125 to 0.125
- block_counts: int32 [32], replicated, may hold values from 1 to 12, 352 in all
- block_offset: int32 [32], replicated, may hold values from 0 to 11
Outputs:
- key_value: bfloat16 [1024, 98304], P('section', 'seq')
The draws below stay inside these ranges and needn't reach their ends.
Inputs may be any that keep to these rules, and one draw needn't show every extreme that they name: `block_counts`: they sum to 352, and the largest is exactly 12.
All inputs are finite; a program needn't handle non-finite values.
Results may differ from the reference program's by a relative error of at most 0.015.
Values may be sent and summed in bfloat16 or wider, within the bound.
A program may use at most 128 MiB of HBM per device.

```python
import math
import jax
import jax.numpy as jnp
import numpy as np
from jax import lax

D = 8192
KVW = 1024
TILE_ROWS = 256
TILE_DEV = 11
S_DEV = 3072
SHARDS = 32
GROUPS = 8
BLOCKS_DEV = 12
MOST = 12
TOKENS = 98304
TILES = 352
VIS_ROWS = 90112


def scaled_field(values, key_rows, key_cols, row_span, rise):
    count = values.shape[0]
    row_scale = jnp.exp(jax.random.uniform(key_rows, (count, 1), minval=0.0, maxval=row_span))
    jitter = jax.random.uniform(key_cols, (D,), minval=0.0, maxval=math.log(4.0))
    col_scale = jnp.exp(rise * jnp.arange(D, dtype=jnp.float32) / D + jitter)
    return (0.05 * values * row_scale * col_scale[None, :]).astype(jnp.bfloat16)


def draw_text_embed(key, part):
    key = jax.random.fold_in(key, 11)
    key_base, key_rows, key_cols = jax.random.split(key, 3)
    gauss_part = jax.random.normal(key_base, (TOKENS, D))
    return scaled_field(gauss_part, key_rows, key_cols, math.log(10.0), math.log(3.0))


def draw_vis_rows(key, part):
    key = jax.random.fold_in(key, 12)
    key_base, key_rows, key_cols = jax.random.split(key, 3)
    gauss_part = jax.random.normal(key_base, (VIS_ROWS, D))
    return scaled_field(gauss_part, key_rows, key_cols, math.log(10.0), math.log(3.0))


def set_ends(array, key, least, largest):
    index_at = [jax.random.randint(jax.random.fold_in(key, axis), (), 0, length) for axis, length in enumerate(array.shape)]
    longest = array.shape.index(max(array.shape))
    beside = index_at[:longest] + [(index_at[longest] + 1) % array.shape[longest]] + index_at[longest + 1:]
    return array.at[tuple(index_at)].set(least).at[tuple(beside)].set(largest)


def spiked(drawn, stream_key, source, target, shards_of, factor):
    owner, partner = [(jnp.arange(drawn.shape[dim]) // (drawn.shape[dim] // shards_of)).reshape([-1 if axis == dim else 1 for axis in range(drawn.ndim)]) for dim in (source, target)]
    chosen = jax.random.permutation(stream_key, shards_of)[partner]
    strong = (owner == chosen) | (owner == (partner + shards_of // 2) % shards_of)
    return jnp.where(strong, factor * drawn, drawn)


def block_scale(rng, extent, shards, low, top_value):
    gain = 1.0
    for position, blocks in shards:
        heights = jax.random.uniform(jax.random.fold_in(jax.random.fold_in(rng, 6), position), (blocks,), jnp.float32, low / len(shards), top_value / len(shards))
        gain = gain * jnp.repeat(jnp.exp(heights), extent[position] // blocks).reshape((-1,) + (1,) * (len(extent) - 1 - position))
    return gain


def split_up(amount, total, most, slope):
    weights = [(1 << 20) // math.isqrt(rank ** slope) + 1 for rank in range(2, amount + 1)]
    spare, given = total - most - (amount - 1), [1] * (amount - 1)
    while spare > 0:
        free = [i for i in range(amount - 1) if given[i] < most]
        pool, budget = sum([weights[i] for i in free]), spare
        for i in free:
            addition = min(most - given[i], max(1, budget * weights[i] // pool), spare)
            given[i] = given[i] + addition
            spare = spare - addition
    return np.array([most] + given)


def ragged_sizes(stream_key, amount, total, bound, slope):
    if amount == 2:
        one = jax.random.randint(stream_key, (), max(1, total - bound), min(bound, total - 1) + 1)
        return jnp.stack([one, total - one])
    tallies = jnp.asarray(split_up(amount, total, bound, slope), jnp.int32)
    pairs = (amount - 1) // 2
    giver, receiver = tallies[1:1 + 2 * pairs:2], tallies[2:2 + 2 * pairs:2]
    room = jnp.minimum(giver - 1, bound - receiver)
    shifted = jax.random.randint(jax.random.fold_in(stream_key, 1), (pairs,), 0, 1 << 20) % (room + 1)
    tallies = tallies.at[1:1 + 2 * pairs:2].set(giver - shifted).at[2:2 + 2 * pairs:2].set(receiver + shifted)
    return tallies[jax.random.permutation(jax.random.fold_in(stream_key, 2), amount)]


def heavy_noise(rng, dims, deviation, bound, shards, heavy, kind=jnp.bfloat16):
    values = deviation * jax.random.normal(rng, dims, jnp.float32)
    if shards:
        values = values * block_scale(rng, dims, shards, -0.22, 0.18)
    return jnp.clip(spiked(values, jax.random.fold_in(rng, 3), *heavy), -bound, bound).astype(kind)


def setup_inputs(seed: int = 0) -> dict:
    streams_of = jax.random.split(jax.random.key(seed), 7)
    return {
        "text_embed": draw_text_embed(jax.random.fold_in(streams_of[6], 71), 0),
        "vis_rows": draw_vis_rows(jax.random.fold_in(streams_of[6], 71), 0),
        "norm_gain": jnp.clip(1.0 + 0.15 * jax.random.normal(streams_of[2], (D,), jnp.float32), 0.25, 1.75).astype(jnp.bfloat16),
        "w_kv": heavy_noise(streams_of[3], (D, KVW), D ** -0.5, 0.125, ((0, 8), (1, 32)), (0, 1, 32, 2.75)),
        "block_counts": ragged_sizes(streams_of[4], SHARDS, TILES, MOST, 2).astype(jnp.int32),
        "block_offset": set_ends(jax.random.randint(streams_of[5], (SHARDS,), 0, BLOCKS_DEV), jax.random.fold_in(streams_of[5], 1), 0, BLOCKS_DEV - 1).astype(jnp.int32),
    }


epsilon = 1e-06

def tile_layout(block_counts, block_offset):
    run_ends = jnp.cumsum(block_counts).astype(jnp.int32)
    run_starts = run_ends - block_counts
    slot_ids = jnp.arange(TILES, dtype=jnp.int32)
    owners = lax.optimization_barrier(jnp.sum((run_ends[None, :] <= slot_ids[:, None]).astype(jnp.int32), axis=1)).astype(jnp.int32)
    order_in = slot_ids - run_starts[owners]
    blocks = (BLOCKS_DEV * owners + (order_in + block_offset[owners]) % BLOCKS_DEV).astype(jnp.int32)
    sources = (TILE_DEV * (slot_ids % SHARDS) + slot_ids // SHARDS).astype(jnp.int32)
    return (blocks, sources)

def reference(text_embed, vis_rows, norm_gain, w_kv, block_counts, block_offset):
    blocks, sources = tile_layout(block_counts, block_offset)
    tile_stack = vis_rows.reshape(TILES, TILE_ROWS, D)[sources]
    merged = text_embed.reshape(SHARDS * BLOCKS_DEV, TILE_ROWS, D).at[blocks].set(tile_stack)
    merged = merged.reshape(SHARDS, S_DEV, D)
    gain_f32 = norm_gain.astype(jnp.float32)
    feat_dev = D // GROUPS

    def one_shard(shard_rows):
        rows_f32 = shard_rows.astype(jnp.float32)
        squares = lax.optimization_barrier(jnp.sum(rows_f32 * rows_f32, axis=1))
        normed = (rows_f32 * lax.rsqrt(squares / D + epsilon)[:, None] * gain_f32).astype(jnp.bfloat16)
        summed = jnp.zeros((S_DEV, KVW), jnp.float32)
        for group_idx in range(GROUPS):
            first_row = group_idx * feat_dev
            partial_sum = jnp.dot(normed[:, first_row:first_row + feat_dev], w_kv[first_row:first_row + feat_dev], preferred_element_type=jnp.float32).astype(jnp.bfloat16)
            partial_sum = lax.optimization_barrier(partial_sum)
            summed = summed + partial_sum.astype(jnp.float32)
        return summed.astype(jnp.bfloat16).T
    stacked = lax.map(one_shard, merged)
    return jnp.transpose(stacked, (1, 0, 2)).reshape(KVW, TOKENS)
```

```python
import functools

import jax
import jax.numpy as jnp
from jax import lax
from jax.experimental import pallas as pl
from jax.experimental.pallas import tpu as pltpu
from jax.sharding import PartitionSpec as P

D = 8192
TILE_ROWS = 256
SLOTS = 352
TILES = 11
BLOCKS = 12
FEAT = 1024
KEYS = 128
MESH = pl.DeviceIdType.MESH
epsilon = 1e-06


def kernel(
    rounds,
    counts,
    offsets,
    text_hbm,
    vis_hbm,
    gain_ref,
    wt_ref,
    out_ref,
    starts,
    x_buf,
    text_buf,
    give_buf,
    got_buf,
    w_buf,
    part,
    near_in,
    last_in,
    near_sum,
    pair_out,
    own_sum,
    pair_in,
    done,
    sq_own,
    sq_all,
    row_scale,
    route_out,
    route_in,
    quad_out,
    final,
    local_sem,
    w_quad_sem,
    w_ring_sem,
    w_mate_sem,
    w_send_sem,
    give_sem,
    sq_sem,
    near_sem,
    last_sem,
    pair_sem,
    step_send_sem,
    route_sem,
    quad_sem,
    text_sem,
):
    total = TILES + rounds
    group = lax.axis_index("section")
    shard = lax.axis_index("seq")
    x_pos, y_hi = lax.rem(group, 4), lax.div(group, 4)
    z_pos, rank = lax.div(shard, 4), lax.rem(shard, 4)
    core = lax.rem(shard, 2)
    half = core
    x_up = y_hi * 4 + lax.rem(x_pos + 1, 4)
    x_down = y_hi * 4 + lax.rem(x_pos + 3, 4)
    y_pair = (1 - y_hi) * 4 + x_pos
    core_mate = z_pos * 4 + rank + 1 - 2 * core

    def quad_mate(step):
        return z_pos * 4 + lax.rem(rank + step, 4)

    def z_mate(step):
        return lax.rem(z_pos + step, 8) * 4 + rank

    def z_at(step):
        return lax.rem(z_pos + step + 8, 8)

    def send(src, dst, send_sem, recv_sem, to_group, to_shard):
        pltpu.make_async_remote_copy(
            src_ref=src,
            dst_ref=dst,
            send_sem=send_sem,
            recv_sem=recv_sem,
            device_id=(to_group, to_shard),
            device_id_type=MESH,
        ).start()

    def wait(ref, sem):
        pltpu.make_async_copy(ref, ref, sem).wait()

    text_copy = pltpu.make_async_copy(text_hbm, text_buf, local_sem.at[0])
    vis_copy = pltpu.make_async_copy(vis_hbm, x_buf.at[pl.ds(0, TILES)], local_sem.at[1])
    text_copy.start()
    vis_copy.start()

    barrier = pltpu.get_barrier_semaphore()

    def greet(to_group, to_shard):
        pl.semaphore_signal(barrier, inc=1, device_id=(to_group, to_shard), device_id_type=MESH)

    for step in range(1, 8):
        greet(lax.rem(group + step, 8), shard)
        greet(group, z_mate(step))
    for step in range(1, 4):
        greet(group, quad_mate(step))

    sq_own[...] = jnp.zeros_like(sq_own)
    w_buf[shard] = (wt_ref[...].astype(jnp.float32) * gain_ref[...].astype(jnp.float32)).astype(jnp.bfloat16)

    def scan(idx, running):
        starts[idx] = running
        return running + counts[idx]

    starts[32] = lax.fori_loop(0, 32, scan, jnp.int32(0))
    my_count, my_offset, my_start = counts[shard], offsets[shard], starts[shard]
    spare_0 = BLOCKS - counts[shard - core]
    spare_1 = BLOCKS - counts[shard - core + 1]
    spare = spare_0 + spare_1
    cut = lax.shift_right_logical(spare + 1, 1)

    pl.semaphore_wait(barrier, 17)

    for step in range(1, 4):
        send(w_buf.at[shard], w_buf.at[shard], w_send_sem, w_quad_sem, group, quad_mate(step))

    text_copy.wait()

    def give(idx, carry):
        number = idx + jnp.where(core == 0, cut, 0)
        give_buf[idx] = text_buf[lax.rem(my_offset + my_count + number, BLOCKS)]
        return carry

    lax.fori_loop(0, rounds, give, 0)
    send(give_buf, got_buf, give_sem.at[0], give_sem.at[1], group, core_mate)

    wait(w_buf.at[pl.ds(0, 3)], w_quad_sem)

    def w_half(quad):
        return w_buf.at[pl.ds(quad * 4 + half * 2, 2)]

    def w_mate_send(quad):
        send(w_half(quad), w_half(quad), w_send_sem, w_mate_sem, group, core_mate)

    def ring_step(step):
        up, down = z_at(1 - step), z_at(step - 1)
        if step < 4:
            send(w_half(up), w_half(up), w_send_sem, w_ring_sem.at[0, step - 1], group, z_mate(1))
            send(w_half(down), w_half(down), w_send_sem, w_ring_sem.at[1, step - 1], group, z_mate(7))
        else:
            up_piece = w_buf.at[up * 4 + half * 2]
            down_piece = w_buf.at[down * 4 + half * 2 + 1]
            send(up_piece, up_piece, w_send_sem, w_ring_sem.at[0, 3], group, z_mate(1))
            send(down_piece, down_piece, w_send_sem, w_ring_sem.at[1, 3], group, z_mate(7))

    def ring_wait(step):
        pieces = 2 if step < 4 else 1
        wait(w_buf.at[pl.ds(0, pieces)], w_ring_sem.at[0, step - 1])
        wait(w_buf.at[pl.ds(0, pieces)], w_ring_sem.at[1, step - 1])

    def squares(idx, carry):
        rows = x_buf[idx].astype(jnp.float32)
        rows = rows * rows
        lanes = rows[:, :128]
        for part_idx in range(1, FEAT // 128):
            lanes = lanes + rows[:, part_idx * 128 : (part_idx + 1) * 128]
        sq_own[pl.ds(idx, 1), :] = jnp.sum(lanes.T, axis=0, keepdims=True)
        return carry

    ring_step(1)
    vis_copy.wait()
    lax.fori_loop(0, 4, squares, 0)
    ring_wait(1)
    ring_step(2)
    w_mate_send(z_at(-1))
    w_mate_send(z_at(1))
    lax.fori_loop(4, 8, squares, 0)
    ring_wait(2)
    ring_step(3)
    w_mate_send(z_at(-2))
    w_mate_send(z_at(2))
    lax.fori_loop(8, TILES, squares, 0)
    ring_wait(3)
    ring_step(4)
    w_mate_send(z_at(-3))
    w_mate_send(z_at(3))

    wait(got_buf, give_sem.at[1])

    def pick(idx, carry):
        number = jnp.maximum(jnp.minimum(idx + core * cut, spare - 1), 0)
        of_first = number < spare_0
        mine = of_first == (core == 0)
        order = jnp.where(of_first, number, number - spare_0)
        here = lax.rem(my_offset + my_count + order, BLOCKS)
        there = jnp.where(core == 0, number - spare_0, number - cut)
        there = jnp.maximum(jnp.minimum(there, rounds - 1), 0)
        x_buf[TILES + idx] = lax.select(mine, text_buf[here], got_buf[there])
        return carry

    lax.fori_loop(0, rounds, pick, 0)
    lax.fori_loop(TILES, total, squares, 0)
    for step in range(1, 8):
        send(sq_own, sq_all.at[group], sq_sem.at[0], sq_sem.at[1], lax.rem(group + step, 8), shard)
    sq_all[group] = sq_own[...]

    ring_wait(4)
    w_mate_send(z_at(4))
    wait(w_buf.at[pl.ds(0, 14)], w_mate_sem)

    far = lax.rem(x_pos + 2, 4)
    up_x = lax.rem(x_pos + 1, 4)
    down_x = lax.rem(x_pos + 3, 4)

    def step_body(step, carry):
        @pl.when(step < total)
        def _():
            rows = x_buf[step]
            res = lax.dot_general(
                w_buf[...].reshape(1024, FEAT),
                rows,
                (((1,), (1,)), ((), ())),
                preferred_element_type=jnp.float32,
            )
            part[step] = res.astype(jnp.bfloat16).reshape(8, KEYS, TILE_ROWS)
            send(part.at[step, 4 + far], near_in.at[step, 0], step_send_sem.at[0], near_sem.at[step], x_up, shard)
            send(part.at[step, far], near_in.at[step, 1], step_send_sem.at[0], near_sem.at[step], x_down, shard)

        @pl.when((step >= 1) & (step <= total))
        def _():
            at = step - 1
            wait(near_in.at[at], near_sem.at[at])
            near_sum[at, 0] = (
                near_in[at, 0].astype(jnp.float32) + part[at, 4 + up_x].astype(jnp.float32)
            ).astype(jnp.bfloat16)
            send(near_sum.at[at, 0], last_in.at[at, 0], step_send_sem.at[1], last_sem.at[at], x_up, shard)
            near_sum[at, 1] = (
                near_in[at, 1].astype(jnp.float32) + part[at, down_x].astype(jnp.float32)
            ).astype(jnp.bfloat16)
            send(near_sum.at[at, 1], last_in.at[at, 1], step_send_sem.at[1], last_sem.at[at], x_down, shard)

        @pl.when(step < total)
        def _():
            send(part.at[step, up_x], last_in.at[step, 2], step_send_sem.at[2], last_sem.at[step], x_up, shard)
            send(part.at[step, 4 + down_x], last_in.at[step, 3], step_send_sem.at[2], last_sem.at[step], x_down, shard)

        @pl.when(step == 2)
        def _():
            wait(sq_all.at[pl.ds(0, 7)], sq_sem.at[1])
            squares_sum = sq_all[0]
            for idx in range(1, 8):
                squares_sum = squares_sum + sq_all[idx]
            row_scale[...] = lax.rsqrt(squares_sum / D + epsilon)

        @pl.when((step >= 2) & (step <= total + 1))
        def _():
            at = step - 2
            wait(last_in.at[at], last_sem.at[at])
            other = 1 - y_hi

            def group_sum(side):
                return (
                    part[at, 4 * side + x_pos].astype(jnp.float32)
                    + last_in[at, 1 - side].astype(jnp.float32)
                    + last_in[at, 2 + side].astype(jnp.float32)
                )

            pair_out[at] = group_sum(other).astype(jnp.bfloat16)
            send(pair_out.at[at], pair_in.at[at], step_send_sem.at[3], pair_sem.at[at], y_pair, shard)
            own_sum[at] = group_sum(y_hi)

        @pl.when(step >= 3)
        def _():
            at = step - 3
            wait(pair_in.at[at], pair_sem.at[at])
            scale = row_scale[pl.ds(at, 1), :]
            summed = own_sum[at] + pair_in[at].astype(jnp.float32)
            done[at] = jnp.where(scale > 0.0, summed * scale, 0.0).astype(jnp.bfloat16)

        @pl.when(step == TILES + 2)
        def _():
            for hop in range(8):
                to = z_at(hop)
                first = jnp.minimum(lax.shift_right_logical(starts[to * 4] - shard + 31, 5), TILES - 1)
                second = jnp.minimum(first + 1, TILES - 1)
                if hop == 0:
                    route_in[z_pos, 0] = done[first]
                    route_in[z_pos, 1] = done[second]
                else:
                    route_out[hop - 1, 0] = done[first]
                    route_out[hop - 1, 1] = done[second]
                    send(route_out.at[hop - 1], route_in.at[z_pos], route_sem.at[0], route_sem.at[1], group, z_mate(hop))

        return carry

    lax.fori_loop(0, total + 3, step_body, 0)

    send(
        done.at[pl.ds(TILES, rounds)],
        final.at[pl.ds(12 + rounds, rounds)],
        text_sem.at[0],
        text_sem.at[1],
        group,
        core_mate,
    )
    for idx in range(rounds):
        final[12 + idx] = done[TILES + idx]

    wait(route_in.at[pl.ds(0, 7)], route_sem.at[1])
    quad_start = starts[z_pos * 4]

    def routed(to, idx):
        begin = starts[z_pos * 4 + to]
        slot = begin + ((rank - begin) & 3) + 4 * idx
        slot = jnp.minimum(slot, SLOTS - 1)
        source = slot & 31
        first = lax.shift_right_logical(quad_start - source + 31, 5)
        place = jnp.maximum(jnp.minimum(lax.shift_right_logical(slot, 5) - first, 1), 0)
        return route_in[lax.shift_right_logical(source, 2), place]

    for step in (2, 3, 1):
        to = lax.rem(rank + step, 4)
        for idx in range(3):
            quad_out[step - 1, idx] = routed(to, idx)
        send(quad_out.at[step - 1], final.at[pl.ds(rank * 3, 3)], quad_sem.at[0], quad_sem.at[1], group, quad_mate(step))
    for idx in range(3):
        final[rank * 3 + idx] = routed(rank, idx)

    wait(final.at[pl.ds(0, 9)], quad_sem.at[1])
    wait(final.at[pl.ds(0, rounds)], text_sem.at[1])

    for block in range(BLOCKS):
        order = lax.rem(block - my_offset + BLOCKS, BLOCKS)
        image = ((my_start + order) & 3) * 3 + lax.shift_right_logical(order, 2)
        number = order - my_count + core * spare_0
        second = number >= cut
        text = jnp.where(second, number - cut, number)
        text = text + jnp.where(second == (core == 1), 12, 12 + rounds)
        place = jnp.where(order < my_count, image, text)
        place = jnp.maximum(jnp.minimum(place, 11 + 2 * rounds), 0)
        out_ref[:, block * TILE_ROWS : (block + 1) * TILE_ROWS] = final[place]

    wait(w_buf.at[pl.ds(0, 31)], w_send_sem)
    wait(got_buf, give_sem.at[0])
    wait(sq_all.at[pl.ds(0, 7)], sq_sem.at[0])
    wait(near_in, step_send_sem.at[0])
    wait(near_sum, step_send_sem.at[1])
    wait(near_in, step_send_sem.at[2])
    wait(pair_in, step_send_sem.at[3])
    wait(route_in.at[pl.ds(0, 7)], route_sem.at[0])
    wait(quad_out, quad_sem.at[0])
    wait(final.at[pl.ds(0, rounds)], text_sem.at[0])


def fast(rounds, collective, text_embed, vis_rows, norm_gain, w_kv, block_counts, block_offset):
    total = TILES + rounds
    padded = -(-total // 8) * 8
    tile = (TILE_ROWS, FEAT)
    keys = (KEYS, TILE_ROWS)
    bf16, f32 = jnp.bfloat16, jnp.float32
    smem = pl.BlockSpec(memory_space=pltpu.SMEM)
    vmem = pl.BlockSpec(memory_space=pltpu.VMEM)
    hbm = pl.BlockSpec(memory_space=pl.ANY)
    dma = pltpu.SemaphoreType.DMA
    return pl.pallas_call(
        functools.partial(kernel, rounds),
        out_shape=jax.ShapeDtypeStruct((KEYS, BLOCKS * TILE_ROWS), bf16),
        in_specs=[smem, smem, hbm, hbm, vmem, vmem],
        out_specs=vmem,
        scratch_shapes=[
            pltpu.SMEM((33,), jnp.int32),
            pltpu.VMEM((total,) + tile, bf16),
            pltpu.VMEM((BLOCKS,) + tile, bf16),
            pltpu.VMEM((rounds,) + tile, bf16),
            pltpu.VMEM((rounds,) + tile, bf16),
            pltpu.VMEM((32, 32, FEAT), bf16),
            pltpu.VMEM((total, 8) + keys, bf16),
            pltpu.VMEM((total, 2) + keys, bf16),
            pltpu.VMEM((total, 4) + keys, bf16),
            pltpu.VMEM((total, 2) + keys, bf16),
            pltpu.VMEM((total,) + keys, bf16),
            pltpu.VMEM((total,) + keys, f32),
            pltpu.VMEM((total,) + keys, bf16),
            pltpu.VMEM((total,) + keys, bf16),
            pltpu.VMEM((padded, TILE_ROWS), f32),
            pltpu.VMEM((8, padded, TILE_ROWS), f32),
            pltpu.VMEM((padded, TILE_ROWS), f32),
            pltpu.VMEM((7, 2) + keys, bf16),
            pltpu.VMEM((8, 2) + keys, bf16),
            pltpu.VMEM((3, 3) + keys, bf16),
            pltpu.VMEM((12 + 2 * rounds,) + keys, bf16),
            dma((2,)),
            dma,
            dma((2, 4)),
            dma,
            dma,
            dma((2,)),
            dma((2,)),
            dma((total,)),
            dma((total,)),
            dma((total,)),
            dma((4,)),
            dma((2,)),
            dma((2,)),
            dma((2,)),
        ],
        compiler_params=pltpu.CompilerParams(
            collective_id=collective,
            has_side_effects=True,
            vmem_limit_bytes=60 * 1024 * 1024,
        ),
        cost_estimate=pl.CostEstimate(flops=2 * total * 256 * 1024 * 1024, bytes_accessed=13 << 20, transcendentals=0),
    )(
        block_counts,
        block_offset,
        text_embed.reshape((BLOCKS,) + tile),
        vis_rows.reshape((TILES,) + tile),
        norm_gain.reshape(1, FEAT),
        w_kv.T,
    )


def slow(text_embed, vis_rows, norm_gain, w_kv, block_counts, block_offset):
    shard_count = lax.axis_size("seq")
    shard_id = lax.axis_index("seq")
    rows_dev, feat_dev = text_embed.shape
    w_full = lax.all_gather(w_kv, "seq", axis=1, tiled=True)
    run_ends = jnp.cumsum(block_counts)
    run_starts = run_ends - block_counts
    slot_ids = shard_id + shard_count * jnp.arange(TILES, dtype=jnp.int32)
    owners = jnp.sum((run_ends[None, :] <= slot_ids[:, None]).astype(jnp.int32), axis=1)
    peer_ids = jnp.arange(shard_count, dtype=jnp.int32)
    send_select = (peer_ids[:, None] == owners[None, :]).astype(jnp.bfloat16)
    order_in = (peer_ids - run_starts[shard_id]) % shard_count
    present = order_in < block_counts[shard_id]
    slot_block = (order_in + block_offset[shard_id]) % BLOCKS
    block_ids = jnp.arange(BLOCKS, dtype=jnp.int32)
    place_select = ((block_ids[:, None] == slot_block[None, :]) & present[None, :]).astype(jnp.bfloat16)
    vision_rows = jnp.repeat(jnp.sum(place_select.astype(jnp.float32), axis=1) > 0.5, TILE_ROWS)
    tile_flat = vis_rows.reshape(TILES, TILE_ROWS * feat_dev)
    outgoing = jnp.dot(send_select, tile_flat, preferred_element_type=jnp.float32).astype(jnp.bfloat16)
    incoming = lax.all_to_all(
        outgoing.reshape(shard_count, TILE_ROWS, feat_dev), "seq", split_axis=0, concat_axis=0, tiled=True
    )
    placed = jnp.dot(
        place_select, incoming.reshape(shard_count, TILE_ROWS * feat_dev), preferred_element_type=jnp.float32
    )
    placed = placed.astype(jnp.bfloat16).reshape(rows_dev, feat_dev)
    merged = jnp.where(vision_rows[:, None], placed, text_embed).astype(jnp.float32)
    squares = lax.psum(jnp.sum(merged * merged, axis=1), "section")
    normed = (merged * lax.rsqrt(squares / D + epsilon)[:, None] * norm_gain.astype(jnp.float32)).astype(jnp.bfloat16)
    term = lax.dot_general(w_full, normed, (((0,), (1,)), ((), ())), preferred_element_type=jnp.float32)
    return lax.psum_scatter(term.astype(jnp.bfloat16), "section", scatter_dimension=0, tiled=True)


ROUNDS = (4, 6)


def local(*args):
    block_counts = args[4]
    spare = 2 * BLOCKS - jnp.sum(block_counts.reshape(16, 2), axis=1)
    needed = jnp.max((spare + 1) // 2)
    branch = sum((needed > rounds).astype(jnp.int32) for rounds in ROUNDS)
    branches = [functools.partial(fast, rounds, idx) for idx, rounds in enumerate(ROUNDS)]
    return lax.switch(branch, branches + [slow], *args)


def solution(mesh):
    return jax.shard_map(
        local,
        mesh=mesh,
        in_specs=(
            P("seq", "section"),
            P("seq", "section"),
            P("section"),
            P("section", "seq"),
            P(),
            P(),
        ),
        out_specs=P("section", "seq"),
        check_vma=False,
    )
```

```python
import functools

import jax
import jax.numpy as jnp
from jax import lax
from jax.experimental import pallas as pl
from jax.experimental.pallas import tpu as pltpu
from jax.sharding import PartitionSpec as P

D = 8192
TILE_ROWS = 256
SLOTS = 352
TILES = 11
BLOCKS = 12
FEAT = 1024
KEYS = 128
MESH = pl.DeviceIdType.MESH
epsilon = 1e-06
X_LAGS = (2, 4, 6)
Y_LAGS = (4, 6, 8)
FIRST_LAST = min(X_LAGS[2], Y_LAGS[2])
LAG = max(X_LAGS[2], Y_LAGS[2])


def kernel(
    rounds,
    counts,
    offsets,
    text_hbm,
    vis_hbm,
    gain_ref,
    wt_ref,
    out_ref,
    starts,
    x_buf,
    text_buf,
    give_buf,
    got_buf,
    w_buf,
    part,
    near_in,
    last_in,
    near_sum,
    pair_out,
    own_sum,
    pair_in,
    half_in,
    half_sum,
    done,
    sq_own,
    sq_all,
    row_scale,
    route_out,
    route_in,
    quad_out,
    final,
    local_sem,
    w_ring_sem,
    w_y_sem,
    w_mate_sem,
    w_send_sem,
    give_sem,
    sq_sem,
    near_sem,
    last_sem,
    pair_sem,
    half_sem,
    step_send_sem,
    route_sem,
    quad_sem,
    text_sem,
):
    total = TILES + rounds
    group = lax.axis_index("section")
    shard = lax.axis_index("seq")
    x_pos, y_hi = lax.rem(group, 4), lax.div(group, 4)
    z_pos, rank = lax.div(shard, 4), lax.rem(shard, 4)
    core = lax.rem(shard, 2)
    turn = 1 - 2 * core
    y_mate_rank = lax.rem(rank + 2, 4)
    x_up = y_hi * 4 + lax.rem(x_pos + 1, 4)
    x_down = y_hi * 4 + lax.rem(x_pos + 3, 4)
    y_pair = (1 - y_hi) * 4 + x_pos
    core_mate = z_pos * 4 + rank + turn

    def quad_mate(step):
        return z_pos * 4 + lax.rem(rank + step, 4)

    def z_at(step):
        return lax.rem(z_pos + step + 8, 8)

    def z_mate(step):
        return z_at(step) * 4 + rank

    def send(src, dst, send_sem, recv_sem, to_group, to_shard):
        pltpu.make_async_remote_copy(
            src_ref=src,
            dst_ref=dst,
            send_sem=send_sem,
            recv_sem=recv_sem,
            device_id=(to_group, to_shard),
            device_id_type=MESH,
        ).start()

    def wait(ref, sem):
        pltpu.make_async_copy(ref, ref, sem).wait()

    text_copy = pltpu.make_async_copy(text_hbm, text_buf, local_sem.at[0])
    vis_copy = pltpu.make_async_copy(vis_hbm, x_buf.at[pl.ds(0, TILES)], local_sem.at[1])
    text_copy.start()
    vis_copy.start()

    barrier = pltpu.get_barrier_semaphore()

    def greet(to_group, to_shard):
        pl.semaphore_signal(barrier, inc=1, device_id=(to_group, to_shard), device_id_type=MESH)

    for step in range(1, 8):
        greet(lax.rem(group + step, 8), shard)
        greet(group, z_mate(step))
    for step in range(1, 4):
        greet(group, quad_mate(step))

    sq_own[...] = jnp.zeros_like(sq_own)
    gain = gain_ref[...].astype(jnp.float32).reshape(1, FEAT)
    w_buf[shard] = (wt_ref[...].astype(jnp.float32) * gain).astype(jnp.bfloat16)

    def scan(idx, running):
        starts[idx] = running
        return running + counts[idx]

    starts[32] = lax.fori_loop(0, 32, scan, jnp.int32(0))
    my_count, my_offset, my_start = counts[shard], offsets[shard], starts[shard]
    spare_0 = BLOCKS - counts[shard - core]
    spare_1 = BLOCKS - counts[shard - core + 1]
    spare = spare_0 + spare_1
    cut = lax.shift_right_logical(spare + 1, 1)

    pl.semaphore_wait(barrier, 17)

    def w_piece(step, stream):
        return w_buf.at[z_at(step) * 4 + (rank, y_mate_rank)[stream]]

    def w_share(step, stream):
        piece = w_piece(step, stream)
        send(piece, piece, w_send_sem, w_mate_sem, group, core_mate)

    def w_pass(step, stream):
        up, down = w_piece(1 - step, stream), w_piece(step - 1, stream)
        if step == 4:
            up, down = up.at[pl.ds(0, 16)], down.at[pl.ds(16, 16)]
        send(up, up, w_send_sem, w_ring_sem.at[stream, 0, step - 1], group, z_mate(1))
        send(down, down, w_send_sem, w_ring_sem.at[stream, 1, step - 1], group, z_mate(7))

    def w_take(step, stream):
        piece = w_buf.at[0] if step < 4 else w_buf.at[0, pl.ds(0, 16)]
        wait(piece, w_ring_sem.at[stream, 0, step - 1])
        wait(piece, w_ring_sem.at[stream, 1, step - 1])
        if step < 4:
            w_pass(step + 1, stream)
            w_share(-step, stream)
        w_share(step, stream)

    own_piece = w_piece(0, 0)
    send(own_piece, own_piece, w_send_sem, w_y_sem, group, quad_mate(2))
    w_pass(1, 0)
    w_share(0, 0)

    text_copy.wait()

    def give(idx, carry):
        number = idx + jnp.where(core == 0, cut, 0)
        give_buf[idx] = text_buf[lax.rem(my_offset + my_count + number, BLOCKS)]
        return carry

    lax.fori_loop(0, rounds, give, 0)
    send(give_buf, got_buf, give_sem.at[0], give_sem.at[1], group, core_mate)

    wait(w_buf.at[0], w_y_sem)
    w_pass(1, 1)
    w_share(0, 1)

    def squares(idx, carry):
        rows = x_buf[idx].astype(jnp.float32)
        rows = rows * rows
        lanes = rows[:, :128]
        for part_idx in range(1, FEAT // 128):
            lanes = lanes + rows[:, part_idx * 128 : (part_idx + 1) * 128]
        sq_own[pl.ds(idx, 1), :] = jnp.sum(lanes.T, axis=0, keepdims=True)
        return carry

    w_take(1, 0)
    vis_copy.wait()
    lax.fori_loop(0, 2, squares, 0)
    w_take(1, 1)
    lax.fori_loop(2, 5, squares, 0)
    w_take(2, 0)
    lax.fori_loop(5, 7, squares, 0)
    w_take(2, 1)
    lax.fori_loop(7, 10, squares, 0)
    w_take(3, 0)
    lax.fori_loop(10, TILES, squares, 0)
    w_take(3, 1)
    wait(got_buf, give_sem.at[1])

    def pick(idx, carry):
        number = jnp.maximum(jnp.minimum(idx + core * cut, spare - 1), 0)
        of_first = number < spare_0
        mine = of_first == (core == 0)
        order = jnp.where(of_first, number, number - spare_0)
        here = lax.rem(my_offset + my_count + order, BLOCKS)
        there = jnp.where(core == 0, number - spare_0, number - cut)
        there = jnp.maximum(jnp.minimum(there, rounds - 1), 0)
        x_buf[TILES + idx] = lax.select(mine, text_buf[here], got_buf[there])
        return carry

    lax.fori_loop(0, rounds, pick, 0)
    lax.fori_loop(TILES, total, squares, 0)
    for step in range(1, 8):
        send(sq_own, sq_all.at[group], sq_sem.at[0], sq_sem.at[1], lax.rem(group + step, 8), shard)
    sq_all[group] = sq_own[...]

    w_take(4, 0)
    w_take(4, 1)
    wait(w_buf.at[pl.ds(0, 16)], w_mate_sem)

    far = lax.rem(x_pos + 2, 4)
    up_x = lax.rem(x_pos + 1, 4)
    down_x = lax.rem(x_pos + 3, 4)
    low, high = pl.ds(0, KEYS // 2), pl.ds(KEYS // 2, KEYS // 2)

    def first_tile(quad):
        least = jnp.maximum(48 * quad - 32, 4 * quad)
        return lax.shift_right_logical(jnp.maximum(least - shard + 31, 0), 5)

    def last_tile(quad):
        most = jnp.minimum(48 * quad + 47, 323 + 4 * quad)
        return jnp.minimum(lax.shift_right_logical(jnp.maximum(most - shard, 0), 5), TILES - 1)

    next_quad = z_at(turn)
    base = jnp.minimum(jnp.where(core == 0, first_tile(next_quad), last_tile(next_quad)), TILES - 1)

    def place_of(tile):
        return lax.rem(turn * (tile - base) + TILES, TILES)

    def tile_at(place):
        return jnp.where(place < TILES, lax.rem(base + turn * place + TILES, TILES), place)

    def ready_at(quad):
        begin, end = first_tile(quad), last_tile(quad)
        ready = jnp.int32(0)
        for idx in range(4):
            tile = jnp.minimum(jnp.minimum(begin + idx, end), TILES - 1)
            ready = jnp.maximum(ready, place_of(tile))
        return ready

    ready = [ready_at(z_at(turn * hop)) for hop in range(8)]

    def routed_from(quad, idx):
        tile = lax.shift_right_logical(starts[quad * 4] - shard + 31, 5) + idx
        return done[place_of(jnp.minimum(tile, TILES - 1))]

    def finish(at, summed):
        scale = row_scale[pl.ds(tile_at(at), 1), :]
        done[at] = jnp.where(scale > 0.0, summed * scale, 0.0).astype(jnp.bfloat16)

    def f32(value):
        return value.astype(jnp.float32)

    def step_body(step, carry):
        def on(lag, kind):
            at = step - lag
            return at, pl.when((at >= 0) & (at < total) & ((at & 1) == kind))

        @pl.when(step < total)
        def _():
            res = lax.dot_general(
                w_buf[...].reshape(1024, FEAT),
                x_buf[tile_at(step)],
                (((1,), (1,)), ((), ())),
                preferred_element_type=jnp.float32,
            )
            part[step] = res.astype(jnp.bfloat16).reshape(8, KEYS, TILE_ROWS)

        at, when = on(0, 0)

        @when
        def _():
            send(part.at[step, 4 + far], near_in.at[step, 0], step_send_sem.at[0], near_sem.at[step], x_up, shard)
            send(part.at[step, far], near_in.at[step, 1], step_send_sem.at[0], near_sem.at[step], x_down, shard)
            send(part.at[step, up_x], last_in.at[step, 2], step_send_sem.at[2], last_sem.at[step], x_up, shard)
            send(part.at[step, 4 + down_x], last_in.at[step, 3], step_send_sem.at[2], last_sem.at[step], x_down, shard)

        at, when = on(0, 1)

        @when
        def _():
            send(
                part.at[step, pl.ds(4 * (1 - y_hi), 4)],
                half_in.at[lax.div(step, 2)],
                step_send_sem.at[4],
                half_sem.at[lax.div(step, 2)],
                y_pair,
                shard,
            )

        @pl.when(step == FIRST_LAST)
        def _():
            wait(sq_all.at[pl.ds(0, 7)], sq_sem.at[1])
            squares_sum = sq_all[0]
            for idx in range(1, 8):
                squares_sum = squares_sum + sq_all[idx]
            row_scale[...] = lax.rsqrt(squares_sum / D + epsilon)

        at_pair, when = on(X_LAGS[2], 0)

        @when
        def _():
            wait(pair_in.at[at_pair], pair_sem.at[at_pair])
            finish(at_pair, own_sum[lax.div(at_pair, 2)] + f32(pair_in[at_pair]))

        at_end, when = on(Y_LAGS[2], 1)

        @when
        def _():
            at, half = at_end, lax.div(at_end, 2)
            wait(last_in.at[at, pl.ds(0, 2)], last_sem.at[at])
            low_sum = f32(half_sum[half, x_pos, low]) + f32(last_in[at, 0, high]) + f32(last_in[at, 1, low])
            high_sum = f32(half_sum[half, x_pos, high]) + f32(last_in[at, 0, low]) + f32(last_in[at, 1, high])
            finish(at, jnp.concatenate([low_sum, high_sum], axis=0))

        at_last, when = on(X_LAGS[1], 0)

        @when
        def _():
            at = at_last
            wait(last_in.at[at], last_sem.at[at])
            other = 1 - y_hi

            def group_sum(side):
                return f32(part[at, 4 * side + x_pos]) + f32(last_in[at, 1 - side]) + f32(last_in[at, 2 + side])

            pair_out[at] = group_sum(other).astype(jnp.bfloat16)
            send(pair_out.at[at], pair_in.at[at], step_send_sem.at[3], pair_sem.at[at], y_pair, shard)
            own_sum[lax.div(at, 2)] = group_sum(y_hi)

        at_near, when = on(X_LAGS[0], 0)

        @when
        def _():
            at = at_near
            wait(near_in.at[at], near_sem.at[at])
            near_sum[at, 0] = (f32(near_in[at, 0]) + f32(part[at, 4 + up_x])).astype(jnp.bfloat16)
            send(near_sum.at[at, 0], last_in.at[at, 0], step_send_sem.at[1], last_sem.at[at], x_up, shard)
            near_sum[at, 1] = (f32(near_in[at, 1]) + f32(part[at, down_x])).astype(jnp.bfloat16)
            send(near_sum.at[at, 1], last_in.at[at, 1], step_send_sem.at[1], last_sem.at[at], x_down, shard)

        at_hop, when = on(Y_LAGS[1], 1)

        @when
        def _():
            at, half = at_hop, lax.div(at_hop, 2)
            wait(near_in.at[at, 0], near_sem.at[at])
            near_sum[at, 0, high] = (f32(near_in[at, 0, high]) + f32(half_sum[half, up_x, high])).astype(jnp.bfloat16)
            near_sum[at, 1, low] = (f32(near_in[at, 0, low]) + f32(half_sum[half, down_x, low])).astype(jnp.bfloat16)
            send(near_sum.at[at, 0, high], last_in.at[at, 0, low], step_send_sem.at[6], last_sem.at[at], x_up, shard)
            send(near_sum.at[at, 1, low], last_in.at[at, 1, low], step_send_sem.at[6], last_sem.at[at], x_down, shard)

        at_half, when = on(Y_LAGS[0], 1)

        @when
        def _():
            at, half = at_half, lax.div(at_half, 2)
            wait(half_in.at[half], half_sem.at[half])
            half_sum[half] = (f32(part[at, pl.ds(4 * y_hi, 4)]) + f32(half_in[half])).astype(jnp.bfloat16)
            send(half_sum.at[half, far, high], near_in.at[at, 0, high], step_send_sem.at[5], near_sem.at[at], x_up, shard)
            send(half_sum.at[half, far, low], near_in.at[at, 0, low], step_send_sem.at[5], near_sem.at[at], x_down, shard)
            send(half_sum.at[half, up_x, low], last_in.at[at, 0, high], step_send_sem.at[5], last_sem.at[at], x_up, shard)
            send(half_sum.at[half, down_x, high], last_in.at[at, 1, high], step_send_sem.at[5], last_sem.at[at], x_down, shard)

        for hop in range(1, 8):
            to = z_at(turn * hop)

            @pl.when(step == ready[hop] + LAG)
            def _():
                route_out[hop - 1, 0] = routed_from(to, 0)
                route_out[hop - 1, 1] = routed_from(to, 1)
                send(route_out.at[hop - 1], route_in.at[z_pos], route_sem.at[0], route_sem.at[1], group, to * 4 + rank)

        return carry

    lax.fori_loop(0, total + LAG, step_body, 0)

    send(
        done.at[pl.ds(TILES, rounds)],
        final.at[pl.ds(12 + rounds, rounds)],
        text_sem.at[0],
        text_sem.at[1],
        group,
        core_mate,
    )
    for idx in range(2):
        route_in[z_pos, idx] = routed_from(z_pos, idx)

    wait(route_in.at[pl.ds(0, 7)], route_sem.at[1])
    quad_start = starts[z_pos * 4]

    def routed(to, idx):
        begin = starts[z_pos * 4 + to]
        slot = begin + ((rank - begin) & 3) + 4 * idx
        slot = jnp.minimum(slot, SLOTS - 1)
        source = slot & 31
        first = lax.shift_right_logical(quad_start - source + 31, 5)
        place = jnp.maximum(jnp.minimum(lax.shift_right_logical(slot, 5) - first, 1), 0)
        return route_in[lax.shift_right_logical(source, 2), place]

    for step in (2, 3, 1):
        to = lax.rem(rank + step, 4)
        for idx in range(3):
            quad_out[step - 1, idx] = routed(to, idx)
        send(quad_out.at[step - 1], final.at[pl.ds(rank * 3, 3)], quad_sem.at[0], quad_sem.at[1], group, quad_mate(step))
    for idx in range(3):
        final[rank * 3 + idx] = routed(rank, idx)
    for idx in range(rounds):
        final[12 + idx] = done[TILES + idx]

    wait(final.at[pl.ds(0, 9)], quad_sem.at[1])
    wait(final.at[pl.ds(0, rounds)], text_sem.at[1])

    for block in range(BLOCKS):
        order = lax.rem(block - my_offset + BLOCKS, BLOCKS)
        image = ((my_start + order) & 3) * 3 + lax.shift_right_logical(order, 2)
        number = order - my_count + core * spare_0
        second = number >= cut
        text = jnp.where(second, number - cut, number)
        text = text + jnp.where(second == (core == 1), 12, 12 + rounds)
        place = jnp.where(order < my_count, image, text)
        place = jnp.maximum(jnp.minimum(place, 11 + 2 * rounds), 0)
        out_ref[:, block * TILE_ROWS : (block + 1) * TILE_ROWS] = final[place]

    evens, odds = (total + 1) // 2, total // 2
    wait(w_buf.at[pl.ds(0, 31)], w_send_sem)
    wait(got_buf, give_sem.at[0])
    wait(sq_all.at[pl.ds(0, 7)], sq_sem.at[0])
    for idx in range(3):
        wait(near_in.at[pl.ds(0, evens)], step_send_sem.at[idx])
    wait(pair_in.at[pl.ds(0, evens)], step_send_sem.at[3])
    wait(half_in, step_send_sem.at[4])
    wait(near_in.at[pl.ds(0, odds)], step_send_sem.at[5])
    wait(pair_in.at[pl.ds(0, odds)], step_send_sem.at[6])
    wait(route_in.at[pl.ds(0, 7)], route_sem.at[0])
    wait(quad_out, quad_sem.at[0])
    wait(final.at[pl.ds(0, rounds)], text_sem.at[0])


def fast(rounds, collective, text_embed, vis_rows, norm_gain, w_kv, block_counts, block_offset):
    total = TILES + rounds
    padded = -(-total // 8) * 8
    tile = (TILE_ROWS, FEAT)
    keys = (KEYS, TILE_ROWS)
    bf16, f32 = jnp.bfloat16, jnp.float32
    smem = pl.BlockSpec(memory_space=pltpu.SMEM)
    vmem = pl.BlockSpec(memory_space=pltpu.VMEM)
    hbm = pl.BlockSpec(memory_space=pl.ANY)
    dma = pltpu.SemaphoreType.DMA
    return pl.pallas_call(
        functools.partial(kernel, rounds),
        out_shape=jax.ShapeDtypeStruct((KEYS, BLOCKS * TILE_ROWS), bf16),
        in_specs=[smem, smem, hbm, hbm, vmem, vmem],
        out_specs=vmem,
        scratch_shapes=[
            pltpu.SMEM((33,), jnp.int32),
            pltpu.VMEM((total,) + tile, bf16),
            pltpu.VMEM((BLOCKS,) + tile, bf16),
            pltpu.VMEM((rounds,) + tile, bf16),
            pltpu.VMEM((rounds,) + tile, bf16),
            pltpu.VMEM((32, 32, FEAT), bf16),
            pltpu.VMEM((total, 8) + keys, bf16),
            pltpu.VMEM((total, 2) + keys, bf16),
            pltpu.VMEM((total, 4) + keys, bf16),
            pltpu.VMEM((total, 2) + keys, bf16),
            pltpu.VMEM((total,) + keys, bf16),
            pltpu.VMEM(((total + 1) // 2,) + keys, f32),
            pltpu.VMEM((total,) + keys, bf16),
            pltpu.VMEM((total // 2, 4) + keys, bf16),
            pltpu.VMEM((total // 2, 4) + keys, bf16),
            pltpu.VMEM((total,) + keys, bf16),
            pltpu.VMEM((padded, TILE_ROWS), f32),
            pltpu.VMEM((8, padded, TILE_ROWS), f32),
            pltpu.VMEM((padded, TILE_ROWS), f32),
            pltpu.VMEM((7, 2) + keys, bf16),
            pltpu.VMEM((8, 2) + keys, bf16),
            pltpu.VMEM((3, 3) + keys, bf16),
            pltpu.VMEM((12 + 2 * rounds,) + keys, bf16),
            dma((2,)),
            dma((2, 2, 4)),
            dma,
            dma,
            dma,
            dma((2,)),
            dma((2,)),
            dma((total,)),
            dma((total,)),
            dma((total,)),
            dma((total // 2,)),
            dma((7,)),
            dma((2,)),
            dma((2,)),
            dma((2,)),
        ],
        compiler_params=pltpu.CompilerParams(
            collective_id=collective,
            has_side_effects=True,
            vmem_limit_bytes=60 * 1024 * 1024,
        ),
        cost_estimate=pl.CostEstimate(flops=2 * total * 256 * 1024 * 1024, bytes_accessed=13 << 20, transcendentals=0),
    )(
        block_counts,
        block_offset,
        text_embed.reshape((BLOCKS,) + tile),
        vis_rows.reshape((TILES,) + tile),
        norm_gain,
        w_kv.T,
    )


def slow(text_embed, vis_rows, norm_gain, w_kv, block_counts, block_offset):
    shard_count = lax.axis_size("seq")
    shard_id = lax.axis_index("seq")
    rows_dev, feat_dev = text_embed.shape
    w_full = lax.all_gather(w_kv, "seq", axis=1, tiled=True)
    run_ends = jnp.cumsum(block_counts)
    run_starts = run_ends - block_counts
    slot_ids = shard_id + shard_count * jnp.arange(TILES, dtype=jnp.int32)
    owners = jnp.sum((run_ends[None, :] <= slot_ids[:, None]).astype(jnp.int32), axis=1)
    peer_ids = jnp.arange(shard_count, dtype=jnp.int32)
    send_select = (peer_ids[:, None] == owners[None, :]).astype(jnp.bfloat16)
    order_in = (peer_ids - run_starts[shard_id]) % shard_count
    present = order_in < block_counts[shard_id]
    slot_block = (order_in + block_offset[shard_id]) % BLOCKS
    block_ids = jnp.arange(BLOCKS, dtype=jnp.int32)
    place_select = ((block_ids[:, None] == slot_block[None, :]) & present[None, :]).astype(jnp.bfloat16)
    vision_rows = jnp.repeat(jnp.sum(place_select.astype(jnp.float32), axis=1) > 0.5, TILE_ROWS)
    tile_flat = vis_rows.reshape(TILES, TILE_ROWS * feat_dev)
    outgoing = jnp.dot(send_select, tile_flat, preferred_element_type=jnp.float32).astype(jnp.bfloat16)
    incoming = lax.all_to_all(
        outgoing.reshape(shard_count, TILE_ROWS, feat_dev), "seq", split_axis=0, concat_axis=0, tiled=True
    )
    placed = jnp.dot(
        place_select, incoming.reshape(shard_count, TILE_ROWS * feat_dev), preferred_element_type=jnp.float32
    )
    placed = placed.astype(jnp.bfloat16).reshape(rows_dev, feat_dev)
    merged = jnp.where(vision_rows[:, None], placed, text_embed).astype(jnp.float32)
    squares = lax.psum(jnp.sum(merged * merged, axis=1), "section")
    normed = (merged * lax.rsqrt(squares / D + epsilon)[:, None] * norm_gain.astype(jnp.float32)).astype(jnp.bfloat16)
    term = lax.dot_general(w_full, normed, (((0,), (1,)), ((), ())), preferred_element_type=jnp.float32)
    return lax.psum_scatter(term.astype(jnp.bfloat16), "section", scatter_dimension=0, tiled=True)


ROUNDS = (4, 6)


def local(*args):
    block_counts = args[4]
    spare = 2 * BLOCKS - jnp.sum(block_counts.reshape(16, 2), axis=1)
    needed = jnp.max((spare + 1) // 2)
    branch = sum((needed > rounds).astype(jnp.int32) for rounds in ROUNDS)
    branches = [functools.partial(fast, rounds, idx) for idx, rounds in enumerate(ROUNDS)]
    return lax.switch(branch, branches + [slow], *args)


def solution(mesh):
    return jax.shard_map(
        local,
        mesh=mesh,
        in_specs=(
            P("seq", "section"),
            P("seq", "section"),
            P("section"),
            P("section", "seq"),
            P(),
            P(),
        ),
        out_specs=P("section", "seq"),
        check_vma=False,
    )
```

```python
import functools

import jax
import jax.numpy as jnp
from jax import lax
from jax.experimental import pallas as pl
from jax.experimental.pallas import tpu as pltpu
from jax.sharding import PartitionSpec as P

D = 8192
TILE_ROWS = 256
SLOTS = 352
TILES = 11
BLOCKS = 12
FEAT = 1024
KEYS = 128
MESH = pl.DeviceIdType.MESH
epsilon = 1e-06
X_LAGS = (2, 4, 6)
Y_LAGS = (3, 5, 7)
FIRST_LAST = min(X_LAGS[2], Y_LAGS[2])
LAG = max(X_LAGS[2], Y_LAGS[2])


def kernel(
    rounds,
    counts,
    offsets,
    text_hbm,
    vis_hbm,
    gain_ref,
    wt_ref,
    out_ref,
    starts,
    x_buf,
    text_buf,
    give_buf,
    got_buf,
    w_buf,
    part,
    near_in,
    last_in,
    near_sum,
    pair_out,
    own_sum,
    pair_in,
    half_in,
    half_sum,
    done,
    sq_own,
    sq_all,
    row_scale,
    route_out,
    route_in,
    quad_out,
    final,
    local_sem,
    w_ring_sem,
    w_y_sem,
    w_mate_sem,
    w_send_sem,
    give_sem,
    sq_sem,
    near_sem,
    last_sem,
    pair_sem,
    half_sem,
    step_send_sem,
    route_sem,
    quad_sem,
    text_sem,
):
    total = TILES + rounds
    group = lax.axis_index("section")
    shard = lax.axis_index("seq")
    x_pos, y_hi = lax.rem(group, 4), lax.div(group, 4)
    z_pos, rank = lax.div(shard, 4), lax.rem(shard, 4)
    core = lax.rem(shard, 2)
    turn = 1 - 2 * core
    y_mate_rank = lax.rem(rank + 2, 4)
    x_up = y_hi * 4 + lax.rem(x_pos + 1, 4)
    x_down = y_hi * 4 + lax.rem(x_pos + 3, 4)
    y_pair = (1 - y_hi) * 4 + x_pos
    core_mate = z_pos * 4 + rank + turn

    def quad_mate(step):
        return z_pos * 4 + lax.rem(rank + step, 4)

    def z_at(step):
        return lax.rem(z_pos + step + 8, 8)

    def z_mate(step):
        return z_at(step) * 4 + rank

    def send(src, dst, send_sem, recv_sem, to_group, to_shard):
        pltpu.make_async_remote_copy(
            src_ref=src,
            dst_ref=dst,
            send_sem=send_sem,
            recv_sem=recv_sem,
            device_id=(to_group, to_shard),
            device_id_type=MESH,
        ).start()

    def wait(ref, sem):
        pltpu.make_async_copy(ref, ref, sem).wait()

    text_copy = pltpu.make_async_copy(text_hbm, text_buf, local_sem.at[0])
    vis_copy = pltpu.make_async_copy(vis_hbm, x_buf.at[pl.ds(0, TILES)], local_sem.at[1])
    text_copy.start()
    vis_copy.start()

    barrier = pltpu.get_barrier_semaphore()

    def greet(to_group, to_shard):
        pl.semaphore_signal(barrier, inc=1, device_id=(to_group, to_shard), device_id_type=MESH)

    for step in range(1, 8):
        greet(lax.rem(group + step, 8), shard)
        greet(group, z_mate(step))
    for step in range(1, 4):
        greet(group, quad_mate(step))

    sq_own[...] = jnp.zeros_like(sq_own)
    gain = gain_ref[...].astype(jnp.float32).reshape(1, FEAT)
    w_buf[shard] = (wt_ref[...].astype(jnp.float32) * gain).astype(jnp.bfloat16)

    def scan(idx, running):
        starts[idx] = running
        return running + counts[idx]

    starts[32] = lax.fori_loop(0, 32, scan, jnp.int32(0))
    my_count, my_start = counts[shard], starts[shard]
    my_offset, skipped = offsets[shard] & 15, lax.shift_right_logical(offsets[shard], 4)
    spare_0 = BLOCKS - counts[shard - core]
    spare_1 = BLOCKS - counts[shard - core + 1]
    spare = spare_0 + spare_1
    cut = lax.shift_right_logical(spare + 1, 1)

    pl.semaphore_wait(barrier, 17)

    def w_piece(step, stream):
        return w_buf.at[z_at(step) * 4 + (rank, y_mate_rank)[stream]]

    def w_share(step, stream):
        piece = w_piece(step, stream)
        send(piece, piece, w_send_sem, w_mate_sem, group, core_mate)

    def w_pass(step, stream):
        up, down = w_piece(1 - step, stream), w_piece(step - 1, stream)
        if step == 4:
            up, down = up.at[pl.ds(0, 16)], down.at[pl.ds(16, 16)]
        send(up, up, w_send_sem, w_ring_sem.at[stream, 0, step - 1], group, z_mate(1))
        send(down, down, w_send_sem, w_ring_sem.at[stream, 1, step - 1], group, z_mate(7))

    def w_take(step, stream):
        piece = w_buf.at[0] if step < 4 else w_buf.at[0, pl.ds(0, 16)]
        wait(piece, w_ring_sem.at[stream, 0, step - 1])
        wait(piece, w_ring_sem.at[stream, 1, step - 1])
        if step < 4:
            w_pass(step + 1, stream)
            w_share(-step, stream)
        w_share(step, stream)

    own_piece = w_piece(0, 0)
    send(own_piece, own_piece, w_send_sem, w_y_sem, group, quad_mate(2))
    w_pass(1, 0)
    w_share(0, 0)

    text_copy.wait()

    def give(idx, carry):
        number = idx + jnp.where(core == 0, cut, 0)
        give_buf[idx] = text_buf[lax.rem(my_offset + my_count + number, BLOCKS)]
        return carry

    lax.fori_loop(0, rounds, give, 0)
    send(give_buf, got_buf, give_sem.at[0], give_sem.at[1], group, core_mate)

    wait(w_buf.at[0], w_y_sem)
    w_pass(1, 1)
    w_share(0, 1)

    def squares(idx, carry):
        rows = x_buf[idx].astype(jnp.float32)
        rows = rows * rows
        lanes = rows[:, :128]
        for part_idx in range(1, FEAT // 128):
            lanes = lanes + rows[:, part_idx * 128 : (part_idx + 1) * 128]
        sq_own[pl.ds(idx, 1), :] = jnp.sum(lanes.T, axis=0, keepdims=True)
        return carry

    w_take(1, 0)
    vis_copy.wait()
    lax.fori_loop(0, 2, squares, 0)
    w_take(1, 1)
    lax.fori_loop(2, 5, squares, 0)
    w_take(2, 0)
    lax.fori_loop(5, 7, squares, 0)
    w_take(2, 1)
    lax.fori_loop(7, 10, squares, 0)
    w_take(3, 0)
    lax.fori_loop(10, TILES, squares, 0)
    w_take(3, 1)
    wait(got_buf, give_sem.at[1])

    def pick(idx, carry):
        number = jnp.maximum(jnp.minimum(idx + skipped + core * cut, spare - 1), 0)
        of_first = number < spare_0
        mine = of_first == (core == 0)
        order = jnp.where(of_first, number, number - spare_0)
        here = lax.rem(my_offset + my_count + order, BLOCKS)
        there = jnp.where(core == 0, number - spare_0, number - cut)
        there = jnp.maximum(jnp.minimum(there, rounds - 1), 0)
        x_buf[TILES + idx] = lax.select(mine, text_buf[here], got_buf[there])
        return carry

    lax.fori_loop(0, rounds, pick, 0)
    lax.fori_loop(TILES, total, squares, 0)
    for step in range(1, 8):
        send(sq_own, sq_all.at[group], sq_sem.at[0], sq_sem.at[1], lax.rem(group + step, 8), shard)
    sq_all[group] = sq_own[...]

    w_take(4, 0)
    w_take(4, 1)
    wait(w_buf.at[pl.ds(0, 16)], w_mate_sem)

    far = lax.rem(x_pos + 2, 4)
    up_x = lax.rem(x_pos + 1, 4)
    down_x = lax.rem(x_pos + 3, 4)
    low, high = pl.ds(0, KEYS // 2), pl.ds(KEYS // 2, KEYS // 2)

    def first_tile(quad):
        least = jnp.maximum(48 * quad - 32, 4 * quad)
        return lax.shift_right_logical(jnp.maximum(least - shard + 31, 0), 5)

    def last_tile(quad):
        most = jnp.minimum(48 * quad + 47, 323 + 4 * quad)
        return jnp.minimum(lax.shift_right_logical(jnp.maximum(most - shard, 0), 5), TILES - 1)

    next_quad = z_at(turn)
    base = jnp.minimum(jnp.where(core == 0, first_tile(next_quad), last_tile(next_quad)), TILES - 1)

    def place_of(tile):
        return lax.rem(turn * (tile - base) + TILES, TILES)

    def tile_at(place):
        return jnp.where(place < TILES, lax.rem(base + turn * place + TILES, TILES), place)

    def ready_at(quad):
        begin, end = first_tile(quad), last_tile(quad)
        ready = jnp.int32(0)
        for idx in range(4):
            tile = jnp.minimum(jnp.minimum(begin + idx, end), TILES - 1)
            ready = jnp.maximum(ready, place_of(tile))
        return ready

    ready = [ready_at(z_at(turn * hop)) for hop in range(8)]

    def routed_from(quad, idx):
        tile = lax.shift_right_logical(starts[quad * 4] - shard + 31, 5) + idx
        return done[place_of(jnp.minimum(tile, TILES - 1))]

    def finish(at, summed):
        scale = row_scale[pl.ds(tile_at(at), 1), :]
        done[at] = jnp.where(scale > 0.0, summed * scale, 0.0).astype(jnp.bfloat16)

        @pl.when(at >= TILES)
        def _():
            final[12 + at - TILES] = done[at]
            send(
                done.at[at], final.at[12 + rounds + at - TILES], text_sem.at[0], text_sem.at[1], group, core_mate
            )

    def f32(value):
        return value.astype(jnp.float32)

    quad_start = starts[z_pos * 4]

    def routed(to, idx):
        begin = starts[z_pos * 4 + to]
        slot = begin + ((rank - begin) & 3) + 4 * idx
        slot = jnp.minimum(slot, SLOTS - 1)
        source = slot & 31
        first = lax.shift_right_logical(quad_start - source + 31, 5)
        place = jnp.maximum(jnp.minimum(lax.shift_right_logical(slot, 5) - first, 1), 0)
        return route_in[lax.shift_right_logical(source, 2), place]

    def quad_exchange():
        for idx in range(2):
            route_in[z_pos, idx] = routed_from(z_pos, idx)
        wait(route_in.at[pl.ds(0, 7)], route_sem.at[1])
        for step in (2, 3, 1):
            to = lax.rem(rank + step, 4)
            for idx in range(3):
                quad_out[step - 1, idx] = routed(to, idx)
            send(
                quad_out.at[step - 1],
                final.at[pl.ds(rank * 3, 3)],
                quad_sem.at[0],
                quad_sem.at[1],
                group,
                quad_mate(step),
            )
        for idx in range(3):
            final[rank * 3 + idx] = routed(rank, idx)

    steps = max(total - 2 + Y_LAGS[2], total + X_LAGS[2])

    def step_body(step, carry):
        def on(lag, kind):
            at = step - lag
            y_first = ((at & 1) == 0) & (at < total - 1)
            return at, pl.when((at >= 0) & (at < total) & (y_first == (kind == 1)))

        @pl.when(step < total)
        def _():
            res = lax.dot_general(
                w_buf[...].reshape(1024, FEAT),
                x_buf[tile_at(step)],
                (((1,), (1,)), ((), ())),
                preferred_element_type=jnp.float32,
            )
            part[step] = res.astype(jnp.bfloat16).reshape(8, KEYS, TILE_ROWS)

        at, when = on(0, 0)

        @when
        def _():
            send(part.at[step, 4 + far], near_in.at[step, 0], step_send_sem.at[0], near_sem.at[step], x_up, shard)
            send(part.at[step, far], near_in.at[step, 1], step_send_sem.at[0], near_sem.at[step], x_down, shard)
            send(part.at[step, up_x], last_in.at[step, 2], step_send_sem.at[2], last_sem.at[step], x_up, shard)
            send(part.at[step, 4 + down_x], last_in.at[step, 3], step_send_sem.at[2], last_sem.at[step], x_down, shard)

        at, when = on(0, 1)

        @when
        def _():
            send(
                part.at[step, pl.ds(4 * (1 - y_hi), 4)],
                half_in.at[lax.div(step, 2)],
                step_send_sem.at[4],
                half_sem.at[lax.div(step, 2)],
                y_pair,
                shard,
            )

        @pl.when(step == steps - 1)
        def _():
            quad_exchange()

        @pl.when(step == FIRST_LAST)
        def _():
            wait(sq_all.at[pl.ds(0, 7)], sq_sem.at[1])
            squares_sum = sq_all[0]
            for idx in range(1, 8):
                squares_sum = squares_sum + sq_all[idx]
            row_scale[...] = lax.rsqrt(squares_sum / D + epsilon)

        at_pair, when = on(X_LAGS[2], 0)

        @when
        def _():
            wait(pair_in.at[at_pair], pair_sem.at[at_pair])
            finish(at_pair, own_sum[lax.div(at_pair, 2)] + f32(pair_in[at_pair]))

        at_end, when = on(Y_LAGS[2], 1)

        @when
        def _():
            at, half = at_end, lax.div(at_end, 2)
            wait(last_in.at[at, pl.ds(0, 2)], last_sem.at[at])
            low_sum = f32(half_sum[half, x_pos, low]) + f32(last_in[at, 0, high]) + f32(last_in[at, 1, low])
            high_sum = f32(half_sum[half, x_pos, high]) + f32(last_in[at, 0, low]) + f32(last_in[at, 1, high])
            finish(at, jnp.concatenate([low_sum, high_sum], axis=0))

        at_last, when = on(X_LAGS[1], 0)

        @when
        def _():
            at = at_last
            wait(last_in.at[at], last_sem.at[at])
            other = 1 - y_hi

            def group_sum(side):
                return f32(part[at, 4 * side + x_pos]) + f32(last_in[at, 1 - side]) + f32(last_in[at, 2 + side])

            pair_out[at] = group_sum(other).astype(jnp.bfloat16)
            send(pair_out.at[at], pair_in.at[at], step_send_sem.at[3], pair_sem.at[at], y_pair, shard)
            own_sum[lax.div(at, 2)] = group_sum(y_hi)

        at_near, when = on(X_LAGS[0], 0)

        @when
        def _():
            at = at_near
            wait(near_in.at[at], near_sem.at[at])
            near_sum[at, 0] = (f32(near_in[at, 0]) + f32(part[at, 4 + up_x])).astype(jnp.bfloat16)
            send(near_sum.at[at, 0], last_in.at[at, 0], step_send_sem.at[1], last_sem.at[at], x_up, shard)
            near_sum[at, 1] = (f32(near_in[at, 1]) + f32(part[at, down_x])).astype(jnp.bfloat16)
            send(near_sum.at[at, 1], last_in.at[at, 1], step_send_sem.at[1], last_sem.at[at], x_down, shard)

        at_hop, when = on(Y_LAGS[1], 1)

        @when
        def _():
            at, half = at_hop, lax.div(at_hop, 2)
            wait(near_in.at[at, 0], near_sem.at[at])
            near_sum[at, 0, high] = (f32(near_in[at, 0, high]) + f32(half_sum[half, up_x, high])).astype(jnp.bfloat16)
            near_sum[at, 1, low] = (f32(near_in[at, 0, low]) + f32(half_sum[half, down_x, low])).astype(jnp.bfloat16)
            send(near_sum.at[at, 0, high], last_in.at[at, 0, low], step_send_sem.at[6], last_sem.at[at], x_up, shard)
            send(near_sum.at[at, 1, low], last_in.at[at, 1, low], step_send_sem.at[6], last_sem.at[at], x_down, shard)

        at_half, when = on(Y_LAGS[0], 1)

        @when
        def _():
            at, half = at_half, lax.div(at_half, 2)
            wait(half_in.at[half], half_sem.at[half])
            half_sum[half] = (f32(part[at, pl.ds(4 * y_hi, 4)]) + f32(half_in[half])).astype(jnp.bfloat16)
            send(half_sum.at[half, far, high], near_in.at[at, 0, high], step_send_sem.at[5], near_sem.at[at], x_up, shard)
            send(half_sum.at[half, far, low], near_in.at[at, 0, low], step_send_sem.at[5], near_sem.at[at], x_down, shard)
            send(half_sum.at[half, up_x, low], last_in.at[at, 0, high], step_send_sem.at[5], last_sem.at[at], x_up, shard)
            send(half_sum.at[half, down_x, high], last_in.at[at, 1, high], step_send_sem.at[5], last_sem.at[at], x_down, shard)

        for hop in range(1, 8):
            to = z_at(turn * hop)

            @pl.when(step == ready[hop] + LAG)
            def _():
                route_out[hop - 1, 0] = routed_from(to, 0)
                route_out[hop - 1, 1] = routed_from(to, 1)
                send(route_out.at[hop - 1], route_in.at[z_pos], route_sem.at[0], route_sem.at[1], group, to * 4 + rank)

        return carry

    lax.fori_loop(0, steps, step_body, 0)

    wait(final.at[pl.ds(0, 9)], quad_sem.at[1])
    wait(final.at[pl.ds(0, rounds)], text_sem.at[1])

    for block in range(BLOCKS):
        order = lax.rem(block - my_offset + BLOCKS, BLOCKS)
        image = ((my_start + order) & 3) * 3 + lax.shift_right_logical(order, 2)
        number = order - my_count + core * spare_0
        second = number >= cut
        text = jnp.where(second, number - cut, number) - skipped
        text = text + jnp.where(second == (core == 1), 12, 12 + rounds)
        place = jnp.where(order < my_count, image, text)
        place = jnp.maximum(jnp.minimum(place, 11 + 2 * rounds), 0)
        out_ref[:, block * TILE_ROWS : (block + 1) * TILE_ROWS] = final[place]

    evens, odds = (total + 1) // 2, total // 2
    wait(w_buf.at[pl.ds(0, 31)], w_send_sem)
    wait(got_buf, give_sem.at[0])
    wait(sq_all.at[pl.ds(0, 7)], sq_sem.at[0])
    for idx in range(3):
        wait(near_in.at[pl.ds(0, evens)], step_send_sem.at[idx])
    wait(pair_in.at[pl.ds(0, evens)], step_send_sem.at[3])
    wait(half_in, step_send_sem.at[4])
    wait(near_in.at[pl.ds(0, odds)], step_send_sem.at[5])
    wait(pair_in.at[pl.ds(0, odds)], step_send_sem.at[6])
    wait(route_in.at[pl.ds(0, 7)], route_sem.at[0])
    wait(quad_out, quad_sem.at[0])
    wait(final.at[pl.ds(0, rounds)], text_sem.at[0])


def fast(rounds, collective, text_embed, vis_rows, norm_gain, w_kv, block_counts, block_offset):
    total = TILES + rounds
    padded = -(-total // 8) * 8
    tile = (TILE_ROWS, FEAT)
    keys = (KEYS, TILE_ROWS)
    bf16, f32 = jnp.bfloat16, jnp.float32
    smem = pl.BlockSpec(memory_space=pltpu.SMEM)
    vmem = pl.BlockSpec(memory_space=pltpu.VMEM)
    hbm = pl.BlockSpec(memory_space=pl.ANY)
    dma = pltpu.SemaphoreType.DMA
    return pl.pallas_call(
        functools.partial(kernel, rounds),
        out_shape=jax.ShapeDtypeStruct((KEYS, BLOCKS * TILE_ROWS), bf16),
        in_specs=[smem, smem, hbm, hbm, vmem, vmem],
        out_specs=vmem,
        scratch_shapes=[
            pltpu.SMEM((33,), jnp.int32),
            pltpu.VMEM((total,) + tile, bf16),
            pltpu.VMEM((BLOCKS,) + tile, bf16),
            pltpu.VMEM((rounds,) + tile, bf16),
            pltpu.VMEM((rounds,) + tile, bf16),
            pltpu.VMEM((32, 32, FEAT), bf16),
            pltpu.VMEM((total, 8) + keys, bf16),
            pltpu.VMEM((total, 2) + keys, bf16),
            pltpu.VMEM((total, 4) + keys, bf16),
            pltpu.VMEM((total, 2) + keys, bf16),
            pltpu.VMEM((total,) + keys, bf16),
            pltpu.VMEM(((total + 1) // 2,) + keys, f32),
            pltpu.VMEM((total,) + keys, bf16),
            pltpu.VMEM((total // 2, 4) + keys, bf16),
            pltpu.VMEM((total // 2, 4) + keys, bf16),
            pltpu.VMEM((total,) + keys, bf16),
            pltpu.VMEM((padded, TILE_ROWS), f32),
            pltpu.VMEM((8, padded, TILE_ROWS), f32),
            pltpu.VMEM((padded, TILE_ROWS), f32),
            pltpu.VMEM((7, 2) + keys, bf16),
            pltpu.VMEM((8, 2) + keys, bf16),
            pltpu.VMEM((3, 3) + keys, bf16),
            pltpu.VMEM((12 + 2 * rounds,) + keys, bf16),
            dma((2,)),
            dma((2, 2, 4)),
            dma,
            dma,
            dma,
            dma((2,)),
            dma((2,)),
            dma((total,)),
            dma((total,)),
            dma((total,)),
            dma((total // 2,)),
            dma((7,)),
            dma((2,)),
            dma((2,)),
            dma((2,)),
        ],
        compiler_params=pltpu.CompilerParams(
            collective_id=collective,
            has_side_effects=True,
            vmem_limit_bytes=60 * 1024 * 1024,
        ),
        cost_estimate=pl.CostEstimate(flops=2 * total * 256 * 1024 * 1024, bytes_accessed=13 << 20, transcendentals=0),
    )(
        block_counts,
        block_offset,
        text_embed.reshape((BLOCKS,) + tile),
        vis_rows.reshape((TILES,) + tile),
        norm_gain,
        w_kv.T,
    )


def slow(text_embed, vis_rows, norm_gain, w_kv, block_counts, block_offset):
    rounds, collective = ROUNDS[-1], len(ROUNDS) - 1
    first, second = [
        fast(rounds, collective, text_embed, vis_rows, norm_gain, w_kv, block_counts, block_offset + 16 * skipped)
        for skipped in (0, rounds)
    ]
    shard = lax.axis_index("seq")
    core = shard % 2
    spare_0 = BLOCKS - block_counts[shard - core]
    cut = (spare_0 + BLOCKS - block_counts[shard - core + 1] + 1) // 2
    order = (jnp.arange(BLOCKS, dtype=jnp.int32) - block_offset[shard]) % BLOCKS
    number = order - block_counts[shard]
    place = number + core * spare_0
    place = jnp.where(place >= cut, place - cut, place)
    late = (number >= 0) & (place >= rounds)
    return jnp.where(jnp.repeat(late, TILE_ROWS)[None, :], second, first)


ROUNDS = (4, 6)


def local(*args):
    block_counts = args[4]
    spare = 2 * BLOCKS - block_counts[:-1] - block_counts[1:]
    spare = jnp.max(jnp.where(jnp.arange(31) % 2 == 0, spare, 0))
    branch = sum((spare > 2 * rounds).astype(jnp.int32) for rounds in ROUNDS)
    branches = [functools.partial(fast, rounds, idx) for idx, rounds in enumerate(ROUNDS)]
    return lax.switch(branch, branches + [slow], *args)


def solution(mesh):
    return jax.shard_map(
        local,
        mesh=mesh,
        in_specs=(
            P("seq", "section"),
            P("seq", "section"),
            P("section"),
            P("section", "seq"),
            P(),
            P(),
        ),
        out_specs=P("section", "seq"),
        check_vma=False,
    )
```

```python
import functools

import jax
import jax.numpy as jnp
from jax import lax
from jax.experimental import pallas as pl
from jax.experimental.pallas import tpu as pltpu
from jax.sharding import PartitionSpec as P

D = 8192
TILE_ROWS = 256
SLOTS = 352
TILES = 11
BLOCKS = 12
FEAT = 1024
KEYS = 128
MESH = pl.DeviceIdType.MESH
epsilon = 1e-06
X_LAGS = (2, 4, 6)
Y_LAGS = (3, 5, 7)
FIRST_LAST = min(X_LAGS[2], Y_LAGS[2])
LAG = max(X_LAGS[2], Y_LAGS[2])


def kernel(
    rounds,
    counts,
    offsets,
    text_hbm,
    vis_hbm,
    gain_ref,
    wt_hbm,
    out_ref,
    starts,
    wt_ref,
    x_buf,
    text_buf,
    give_buf,
    got_buf,
    w_buf,
    part,
    near_in,
    last_in,
    near_sum,
    pair_out,
    own_sum,
    pair_in,
    half_in,
    half_sum,
    done,
    sq_own,
    sq_all,
    row_scale,
    route_out,
    route_in,
    quad_out,
    final,
    local_sem,
    w_ring_sem,
    w_y_sem,
    w_mate_sem,
    w_send_sem,
    give_sem,
    sq_sem,
    near_sem,
    last_sem,
    pair_sem,
    half_sem,
    step_send_sem,
    route_sem,
    quad_sem,
    text_sem,
):
    total = TILES + rounds
    group = lax.axis_index("section")
    shard = lax.axis_index("seq")
    x_pos, y_hi = lax.rem(group, 4), lax.div(group, 4)
    z_pos, rank = lax.div(shard, 4), lax.rem(shard, 4)
    core = lax.rem(shard, 2)
    turn = 1 - 2 * core
    y_mate_rank = lax.rem(rank + 2, 4)
    x_up = y_hi * 4 + lax.rem(x_pos + 1, 4)
    x_down = y_hi * 4 + lax.rem(x_pos + 3, 4)
    y_pair = (1 - y_hi) * 4 + x_pos
    core_mate = z_pos * 4 + rank + turn

    def quad_mate(step):
        return z_pos * 4 + lax.rem(rank + step, 4)

    def z_at(step):
        return lax.rem(z_pos + step + 8, 8)

    def z_mate(step):
        return z_at(step) * 4 + rank

    def send(src, dst, send_sem, recv_sem, to_group, to_shard):
        pltpu.make_async_remote_copy(
            src_ref=src,
            dst_ref=dst,
            send_sem=send_sem,
            recv_sem=recv_sem,
            device_id=(to_group, to_shard),
            device_id_type=MESH,
        ).start()

    def wait(ref, sem):
        pltpu.make_async_copy(ref, ref, sem).wait()

    text_copy = pltpu.make_async_copy(text_hbm, text_buf, local_sem.at[0])
    vis_copy = pltpu.make_async_copy(vis_hbm, x_buf.at[pl.ds(0, TILES)], local_sem.at[1])
    wt_copy = pltpu.make_async_copy(wt_hbm, wt_ref, local_sem.at[2])
    wt_copy.start()
    text_copy.start()
    vis_copy.start()

    barrier = pltpu.get_barrier_semaphore()

    def greet(to_group, to_shard):
        pl.semaphore_signal(barrier, inc=1, device_id=(to_group, to_shard), device_id_type=MESH)

    for step in range(1, 8):
        greet(lax.rem(group + step, 8), shard)
        greet(group, z_mate(step))
    for step in range(1, 4):
        greet(group, quad_mate(step))

    sq_own[...] = jnp.zeros_like(sq_own)
    gain = gain_ref[...].astype(jnp.float32).reshape(1, FEAT)
    wt_copy.wait()
    w_buf[shard] = (wt_ref[...].astype(jnp.float32) * gain).astype(jnp.bfloat16)

    def scan(idx, running):
        starts[idx] = running
        return running + counts[idx]

    starts[32] = lax.fori_loop(0, 32, scan, jnp.int32(0))
    my_count, my_start = counts[shard], starts[shard]
    my_offset, skipped = offsets[shard] & 15, lax.shift_right_logical(offsets[shard], 4)
    spare_0 = BLOCKS - counts[shard - core]
    spare_1 = BLOCKS - counts[shard - core + 1]
    spare = spare_0 + spare_1
    cut = lax.shift_right_logical(spare + 1, 1)

    pl.semaphore_wait(barrier, 17)

    def w_piece(step, stream):
        return w_buf.at[z_at(step) * 4 + (rank, y_mate_rank)[stream]]

    def w_share(step, stream):
        piece = w_piece(step, stream)
        send(piece, piece, w_send_sem, w_mate_sem, group, core_mate)

    def w_pass(step, stream):
        up, down = w_piece(1 - step, stream), w_piece(step - 1, stream)
        if step == 4:
            up, down = up.at[pl.ds(0, 16)], down.at[pl.ds(16, 16)]
        send(up, up, w_send_sem, w_ring_sem.at[stream, 0, step - 1], group, z_mate(1))
        send(down, down, w_send_sem, w_ring_sem.at[stream, 1, step - 1], group, z_mate(7))

    def w_take(step, stream):
        piece = w_buf.at[0] if step < 4 else w_buf.at[0, pl.ds(0, 16)]
        wait(piece, w_ring_sem.at[stream, 0, step - 1])
        wait(piece, w_ring_sem.at[stream, 1, step - 1])
        if step < 4:
            w_pass(step + 1, stream)
            w_share(-step, stream)
        w_share(step, stream)

    own_piece = w_piece(0, 0)
    send(own_piece, own_piece, w_send_sem, w_y_sem, group, quad_mate(2))
    w_pass(1, 0)
    w_share(0, 0)

    text_copy.wait()

    def give(idx, carry):
        number = idx + jnp.where(core == 0, cut, 0)
        give_buf[idx] = text_buf[lax.rem(my_offset + my_count + number, BLOCKS)]
        return carry

    lax.fori_loop(0, rounds, give, 0)
    send(give_buf, got_buf, give_sem.at[0], give_sem.at[1], group, core_mate)

    wait(w_buf.at[0], w_y_sem)
    w_pass(1, 1)
    w_share(0, 1)

    def squares(idx, carry):
        rows = x_buf[idx].astype(jnp.float32)
        rows = rows * rows
        lanes = rows[:, :128]
        for part_idx in range(1, FEAT // 128):
            lanes = lanes + rows[:, part_idx * 128 : (part_idx + 1) * 128]
        sq_own[pl.ds(idx, 1), :] = jnp.sum(lanes.T, axis=0, keepdims=True)
        return carry

    w_take(1, 0)
    vis_copy.wait()
    lax.fori_loop(0, 2, squares, 0)
    w_take(1, 1)
    lax.fori_loop(2, 5, squares, 0)
    w_take(2, 0)
    lax.fori_loop(5, 7, squares, 0)
    w_take(2, 1)
    lax.fori_loop(7, 10, squares, 0)
    w_take(3, 0)
    lax.fori_loop(10, TILES, squares, 0)
    w_take(3, 1)
    wait(got_buf, give_sem.at[1])

    def pick(idx, carry):
        number = jnp.maximum(jnp.minimum(idx + skipped + core * cut, spare - 1), 0)
        of_first = number < spare_0
        mine = of_first == (core == 0)
        order = jnp.where(of_first, number, number - spare_0)
        here = lax.rem(my_offset + my_count + order, BLOCKS)
        there = jnp.where(core == 0, number - spare_0, number - cut)
        there = jnp.maximum(jnp.minimum(there, rounds - 1), 0)
        x_buf[TILES + idx] = lax.select(mine, text_buf[here], got_buf[there])
        return carry

    lax.fori_loop(0, rounds, pick, 0)
    lax.fori_loop(TILES, total, squares, 0)
    for step in range(1, 8):
        send(sq_own, sq_all.at[group], sq_sem.at[0], sq_sem.at[1], lax.rem(group + step, 8), shard)
    sq_all[group] = sq_own[...]

    w_take(4, 0)
    w_take(4, 1)
    wait(w_buf.at[pl.ds(0, 16)], w_mate_sem)

    far = lax.rem(x_pos + 2, 4)
    up_x = lax.rem(x_pos + 1, 4)
    down_x = lax.rem(x_pos + 3, 4)
    low, high = pl.ds(0, KEYS // 2), pl.ds(KEYS // 2, KEYS // 2)

    def first_tile(quad):
        least = jnp.maximum(48 * quad - 32, 4 * quad)
        return lax.shift_right_logical(jnp.maximum(least - shard + 31, 0), 5)

    def last_tile(quad):
        most = jnp.minimum(48 * quad + 47, 323 + 4 * quad)
        return jnp.minimum(lax.shift_right_logical(jnp.maximum(most - shard, 0), 5), TILES - 1)

    next_quad = z_at(turn)
    base = jnp.minimum(jnp.where(core == 0, first_tile(next_quad), last_tile(next_quad)), TILES - 1)

    def place_of(tile):
        return lax.rem(turn * (tile - base) + TILES, TILES)

    def tile_at(place):
        return jnp.where(place < TILES, lax.rem(base + turn * place + TILES, TILES), place)

    def ready_at(quad):
        begin, end = first_tile(quad), last_tile(quad)
        ready = jnp.int32(0)
        for idx in range(4):
            tile = jnp.minimum(jnp.minimum(begin + idx, end), TILES - 1)
            ready = jnp.maximum(ready, place_of(tile))
        return ready

    ready = [ready_at(z_at(turn * hop)) for hop in range(8)]

    def routed_from(quad, idx):
        tile = lax.shift_right_logical(starts[quad * 4] - shard + 31, 5) + idx
        return done[place_of(jnp.minimum(tile, TILES - 1))]

    def finish(at, summed):
        scale = row_scale[pl.ds(tile_at(at), 1), :]
        done[at] = jnp.where(scale > 0.0, summed * scale, 0.0).astype(jnp.bfloat16)

        @pl.when(at >= TILES)
        def _():
            final[12 + at - TILES] = done[at]
            send(
                done.at[at], final.at[12 + rounds + at - TILES], text_sem.at[0], text_sem.at[1], group, core_mate
            )

    def f32(value):
        return value.astype(jnp.float32)

    quad_start = starts[z_pos * 4]

    def routed(to, idx):
        begin = starts[z_pos * 4 + to]
        slot = begin + ((rank - begin) & 3) + 4 * idx
        slot = jnp.minimum(slot, SLOTS - 1)
        source = slot & 31
        first = lax.shift_right_logical(quad_start - source + 31, 5)
        place = jnp.maximum(jnp.minimum(lax.shift_right_logical(slot, 5) - first, 1), 0)
        return route_in[lax.shift_right_logical(source, 2), place]

    def quad_exchange():
        for idx in range(2):
            route_in[z_pos, idx] = routed_from(z_pos, idx)
        wait(route_in.at[pl.ds(0, 7)], route_sem.at[1])
        for step in (2, 3, 1):
            to = lax.rem(rank + step, 4)
            for idx in range(3):
                quad_out[step - 1, idx] = routed(to, idx)
            send(
                quad_out.at[step - 1],
                final.at[pl.ds(rank * 3, 3)],
                quad_sem.at[0],
                quad_sem.at[1],
                group,
                quad_mate(step),
            )
        for idx in range(3):
            final[rank * 3 + idx] = routed(rank, idx)

    steps = max(total - 2 + Y_LAGS[2], total + X_LAGS[2])

    def step_body(step, carry):
        def on(lag, kind):
            at = step - lag
            y_first = ((at & 1) == 0) & (at < total - 1)
            return at, pl.when((at >= 0) & (at < total) & (y_first == (kind == 1)))

        @pl.when(step < total)
        def _():
            res = lax.dot_general(
                w_buf[...].reshape(1024, FEAT),
                x_buf[tile_at(step)],
                (((1,), (1,)), ((), ())),
                preferred_element_type=jnp.float32,
            )
            part[step] = res.astype(jnp.bfloat16).reshape(8, KEYS, TILE_ROWS)

        at, when = on(0, 0)

        @when
        def _():
            send(part.at[step, 4 + far], near_in.at[step, 0], step_send_sem.at[0], near_sem.at[step], x_up, shard)
            send(part.at[step, far], near_in.at[step, 1], step_send_sem.at[0], near_sem.at[step], x_down, shard)
            send(part.at[step, up_x], last_in.at[step, 2], step_send_sem.at[2], last_sem.at[step], x_up, shard)
            send(part.at[step, 4 + down_x], last_in.at[step, 3], step_send_sem.at[2], last_sem.at[step], x_down, shard)

        at, when = on(0, 1)

        @when
        def _():
            send(
                part.at[step, pl.ds(4 * (1 - y_hi), 4)],
                half_in.at[lax.div(step, 2)],
                step_send_sem.at[4],
                half_sem.at[lax.div(step, 2)],
                y_pair,
                shard,
            )

        @pl.when(step == steps - 1)
        def _():
            quad_exchange()

        @pl.when(step == FIRST_LAST)
        def _():
            wait(sq_all.at[pl.ds(0, 7)], sq_sem.at[1])
            squares_sum = sq_all[0]
            for idx in range(1, 8):
                squares_sum = squares_sum + sq_all[idx]
            row_scale[...] = lax.rsqrt(squares_sum / D + epsilon)

        at_pair, when = on(X_LAGS[2], 0)

        @when
        def _():
            wait(pair_in.at[at_pair], pair_sem.at[at_pair])
            finish(at_pair, own_sum[lax.div(at_pair, 2)] + f32(pair_in[at_pair]))

        at_end, when = on(Y_LAGS[2], 1)

        @when
        def _():
            at, half = at_end, lax.div(at_end, 2)
            wait(last_in.at[at, pl.ds(0, 2)], last_sem.at[at])
            low_sum = f32(half_sum[half, x_pos, low]) + f32(last_in[at, 0, high]) + f32(last_in[at, 1, low])
            high_sum = f32(half_sum[half, x_pos, high]) + f32(last_in[at, 0, low]) + f32(last_in[at, 1, high])
            finish(at, jnp.concatenate([low_sum, high_sum], axis=0))

        at_last, when = on(X_LAGS[1], 0)

        @when
        def _():
            at = at_last
            wait(last_in.at[at], last_sem.at[at])
            other = 1 - y_hi

            def group_sum(side):
                return f32(part[at, 4 * side + x_pos]) + f32(last_in[at, 1 - side]) + f32(last_in[at, 2 + side])

            pair_out[at] = group_sum(other).astype(jnp.bfloat16)
            send(pair_out.at[at], pair_in.at[at], step_send_sem.at[3], pair_sem.at[at], y_pair, shard)
            own_sum[lax.div(at, 2)] = group_sum(y_hi)

        at_near, when = on(X_LAGS[0], 0)

        @when
        def _():
            at = at_near
            wait(near_in.at[at], near_sem.at[at])
            near_sum[at, 0] = (f32(near_in[at, 0]) + f32(part[at, 4 + up_x])).astype(jnp.bfloat16)
            send(near_sum.at[at, 0], last_in.at[at, 0], step_send_sem.at[1], last_sem.at[at], x_up, shard)
            near_sum[at, 1] = (f32(near_in[at, 1]) + f32(part[at, down_x])).astype(jnp.bfloat16)
            send(near_sum.at[at, 1], last_in.at[at, 1], step_send_sem.at[1], last_sem.at[at], x_down, shard)

        at_hop, when = on(Y_LAGS[1], 1)

        @when
        def _():
            at, half = at_hop, lax.div(at_hop, 2)
            wait(near_in.at[at, 0], near_sem.at[at])
            near_sum[at, 0, high] = (f32(near_in[at, 0, high]) + f32(half_sum[half, up_x, high])).astype(jnp.bfloat16)
            near_sum[at, 1, low] = (f32(near_in[at, 0, low]) + f32(half_sum[half, down_x, low])).astype(jnp.bfloat16)
            send(near_sum.at[at, 0, high], last_in.at[at, 0, low], step_send_sem.at[6], last_sem.at[at], x_up, shard)
            send(near_sum.at[at, 1, low], last_in.at[at, 1, low], step_send_sem.at[6], last_sem.at[at], x_down, shard)

        at_half, when = on(Y_LAGS[0], 1)

        @when
        def _():
            at, half = at_half, lax.div(at_half, 2)
            wait(half_in.at[half], half_sem.at[half])
            half_sum[half] = (f32(part[at, pl.ds(4 * y_hi, 4)]) + f32(half_in[half])).astype(jnp.bfloat16)
            send(half_sum.at[half, far, high], near_in.at[at, 0, high], step_send_sem.at[5], near_sem.at[at], x_up, shard)
            send(half_sum.at[half, far, low], near_in.at[at, 0, low], step_send_sem.at[5], near_sem.at[at], x_down, shard)
            send(half_sum.at[half, up_x, low], last_in.at[at, 0, high], step_send_sem.at[5], last_sem.at[at], x_up, shard)
            send(half_sum.at[half, down_x, high], last_in.at[at, 1, high], step_send_sem.at[5], last_sem.at[at], x_down, shard)

        for hop in range(1, 8):
            to = z_at(turn * hop)

            @pl.when(step == ready[hop] + LAG)
            def _():
                route_out[hop - 1, 0] = routed_from(to, 0)
                route_out[hop - 1, 1] = routed_from(to, 1)
                send(route_out.at[hop - 1], route_in.at[z_pos], route_sem.at[0], route_sem.at[1], group, to * 4 + rank)

        return carry

    lax.fori_loop(0, steps, step_body, 0)

    wait(final.at[pl.ds(0, 9)], quad_sem.at[1])
    wait(final.at[pl.ds(0, rounds)], text_sem.at[1])

    for block in range(BLOCKS):
        order = lax.rem(block - my_offset + BLOCKS, BLOCKS)
        image = ((my_start + order) & 3) * 3 + lax.shift_right_logical(order, 2)
        number = order - my_count + core * spare_0
        second = number >= cut
        text = jnp.where(second, number - cut, number) - skipped
        text = text + jnp.where(second == (core == 1), 12, 12 + rounds)
        place = jnp.where(order < my_count, image, text)
        place = jnp.maximum(jnp.minimum(place, 11 + 2 * rounds), 0)
        out_ref[:, block * TILE_ROWS : (block + 1) * TILE_ROWS] = final[place]

    evens, odds = (total + 1) // 2, total // 2
    wait(w_buf.at[pl.ds(0, 31)], w_send_sem)
    wait(got_buf, give_sem.at[0])
    wait(sq_all.at[pl.ds(0, 7)], sq_sem.at[0])
    for idx in range(3):
        wait(near_in.at[pl.ds(0, evens)], step_send_sem.at[idx])
    wait(pair_in.at[pl.ds(0, evens)], step_send_sem.at[3])
    wait(half_in, step_send_sem.at[4])
    wait(near_in.at[pl.ds(0, odds)], step_send_sem.at[5])
    wait(pair_in.at[pl.ds(0, odds)], step_send_sem.at[6])
    wait(route_in.at[pl.ds(0, 7)], route_sem.at[0])
    wait(quad_out, quad_sem.at[0])
    wait(final.at[pl.ds(0, rounds)], text_sem.at[0])


def fast(rounds, collective, text_embed, vis_rows, norm_gain, w_kv, block_counts, block_offset):
    total = TILES + rounds
    padded = -(-total // 8) * 8
    tile = (TILE_ROWS, FEAT)
    keys = (KEYS, TILE_ROWS)
    bf16, f32 = jnp.bfloat16, jnp.float32
    smem = pl.BlockSpec(memory_space=pltpu.SMEM)
    vmem = pl.BlockSpec(memory_space=pltpu.VMEM)
    hbm = pl.BlockSpec(memory_space=pl.ANY)
    dma = pltpu.SemaphoreType.DMA
    return pl.pallas_call(
        functools.partial(kernel, rounds),
        out_shape=jax.ShapeDtypeStruct((KEYS, BLOCKS * TILE_ROWS), bf16),
        in_specs=[smem, smem, hbm, hbm, vmem, hbm],
        out_specs=vmem,
        scratch_shapes=[
            pltpu.SMEM((33,), jnp.int32),
            pltpu.VMEM((32, FEAT), bf16),
            pltpu.VMEM((total,) + tile, bf16),
            pltpu.VMEM((BLOCKS,) + tile, bf16),
            pltpu.VMEM((rounds,) + tile, bf16),
            pltpu.VMEM((rounds,) + tile, bf16),
            pltpu.VMEM((32, 32, FEAT), bf16),
            pltpu.VMEM((total, 8) + keys, bf16),
            pltpu.VMEM((total, 2) + keys, bf16),
            pltpu.VMEM((total, 4) + keys, bf16),
            pltpu.VMEM((total, 2) + keys, bf16),
            pltpu.VMEM((total,) + keys, bf16),
            pltpu.VMEM(((total + 1) // 2,) + keys, f32),
            pltpu.VMEM((total,) + keys, bf16),
            pltpu.VMEM((total // 2, 4) + keys, bf16),
            pltpu.VMEM((total // 2, 4) + keys, bf16),
            pltpu.VMEM((total,) + keys, bf16),
            pltpu.VMEM((padded, TILE_ROWS), f32),
            pltpu.VMEM((8, padded, TILE_ROWS), f32),
            pltpu.VMEM((padded, TILE_ROWS), f32),
            pltpu.VMEM((7, 2) + keys, bf16),
            pltpu.VMEM((8, 2) + keys, bf16),
            pltpu.VMEM((3, 3) + keys, bf16),
            pltpu.VMEM((12 + 2 * rounds,) + keys, bf16),
            dma((3,)),
            dma((2, 2, 4)),
            dma,
            dma,
            dma,
            dma((2,)),
            dma((2,)),
            dma((total,)),
            dma((total,)),
            dma((total,)),
            dma((total // 2,)),
            dma((7,)),
            dma((2,)),
            dma((2,)),
            dma((2,)),
        ],
        compiler_params=pltpu.CompilerParams(
            collective_id=collective,
            has_side_effects=True,
            vmem_limit_bytes=60 * 1024 * 1024,
        ),
        cost_estimate=pl.CostEstimate(flops=2 * total * 256 * 1024 * 1024, bytes_accessed=13 << 20, transcendentals=0),
    )(
        block_counts,
        block_offset,
        text_embed.reshape((BLOCKS,) + tile),
        vis_rows.reshape((TILES,) + tile),
        norm_gain,
        w_kv.T,
    )


def slow(text_embed, vis_rows, norm_gain, w_kv, block_counts, block_offset):
    rounds, collective = ROUNDS[-1], len(ROUNDS) - 1
    first, second = [
        fast(rounds, collective, text_embed, vis_rows, norm_gain, w_kv, block_counts, block_offset + 16 * skipped)
        for skipped in (0, rounds)
    ]
    shard = lax.axis_index("seq")
    core = shard % 2
    spare_0 = BLOCKS - block_counts[shard - core]
    cut = (spare_0 + BLOCKS - block_counts[shard - core + 1] + 1) // 2
    order = (jnp.arange(BLOCKS, dtype=jnp.int32) - block_offset[shard]) % BLOCKS
    number = order - block_counts[shard]
    place = number + core * spare_0
    place = jnp.where(place >= cut, place - cut, place)
    late = (number >= 0) & (place >= rounds)
    return jnp.where(jnp.repeat(late, TILE_ROWS)[None, :], second, first)


ROUNDS = (4, 6)


def local(*args):
    block_counts = args[4]
    spare = 2 * BLOCKS - block_counts[:-1] - block_counts[1:]
    spare = jnp.max(jnp.where(jnp.arange(31) % 2 == 0, spare, 0))
    branch = sum((spare > 2 * rounds).astype(jnp.int32) for rounds in ROUNDS)
    branches = [functools.partial(fast, rounds, idx) for idx, rounds in enumerate(ROUNDS)]
    return lax.switch(branch, branches + [slow], *args)


def solution(mesh):
    return jax.shard_map(
        local,
        mesh=mesh,
        in_specs=(
            P("seq", "section"),
            P("seq", "section"),
            P("section"),
            P("section", "seq"),
            P(),
            P(),
        ),
        out_specs=P("section", "seq"),
        check_vma=False,
    )
```
